512 devices in a mesh: ctx: 128 (over z, y, core), head: 4 (over x).
Axes of the slice: x: 4, y: 4, z: 16, core: 2. Of those that a mesh axis runs over, the one named last changes fastest.
Arguments:
- queries: bfloat16 [65536, 1024], P('ctx', 'head'), parts along dimension 1, may hold values from -100 to 100
- keys: bfloat16 [65536, 1024], P('ctx', 'head'), parts along dimension 1, may hold values from -5 to 5
- values: bfloat16 [65536, 1024], P('ctx', 'head'), parts along dimension 1, may hold values from -5 to 5
Outputs:
- attended: bfloat16 [65536, 1024], P('ctx', 'head'), parts along dimension 1
The draws below stay inside these ranges and needn't reach their ends.
There are 4 independent parts, one for each index of `head`. The reference program is written for one: setup_inputs(seed, part) draws one part's arguments, and reference() takes and returns one part's arrays. A program takes and returns all parts, laid end to end along the dimension named above; each array names one. Nothing has to cross between parts.
All inputs are finite; a program needn't handle non-finite values.
Results may differ from the reference program's by a relative error of at most 0.001.
Values sent between devices are 32-bit elements; how exact they have to be, the bound alone decides.
A program may use at most 64 MiB of HBM per device.

```python
import math
import jax
import jax.numpy as jnp
from jax import lax

NB = 128
HEADS = 2
DH = 128
TOKENS = 65536


def periodic(key, channels):
    spans = max((TOKENS // NB).bit_length() - 1, 1)
    key_len, key_oct, key_off, key_amp = jax.random.split(key, 4)
    base_len = 2 * NB + jax.random.randint(key_len, (channels,), 0, 2 * NB)
    octave = jax.random.randint(key_oct, (channels,), 0, spans)
    period = base_len * jnp.power(2, octave)
    offset = jax.random.randint(key_off, (channels,), 0, 2 ** 20) % period
    amplitude = jnp.exp(jax.random.uniform(key_amp, (channels,), minval=math.log(0.3), maxval=math.log(1.5)))
    where = jnp.arange(TOKENS, dtype=jnp.int32)[:, None]
    turn = ((where + offset[None, :]) % period[None, :]).astype(jnp.float32) / period.astype(jnp.float32)[None, :]
    return amplitude[None, :] * jnp.sin(2.0 * math.pi * turn)


def key_rows(key, spread):
    shared = periodic(jax.random.fold_in(key, 101), HEADS * DH)
    noise_key = jax.random.fold_in(key, 102)
    noise = spread[1] * jax.random.truncated_normal(noise_key, -4.0, 4.0, (TOKENS, HEADS * DH))
    rows = shared + noise
    where = jnp.arange(TOKENS, dtype=jnp.int32)[:, None]
    twin = (where % 1024 == 43) & (spread[2] > 0.5)
    return (shared, jnp.where(twin, 1.02 * jnp.roll(rows, 1, axis=0), rows))


def draw_keys(key, part):
    shared, rows = key_rows(key, (0.0, 0.8, 0.0))
    return rows.astype(jnp.bfloat16)


def draw_queries(key, part):
    shared, rows = key_rows(key, (0.0, 0.8, 0.0))
    key = jax.random.fold_in(key, 5)
    own = shared + 0.8 * jax.random.truncated_normal(key, -4.0, 4.0, (TOKENS, HEADS * DH))
    return jnp.clip(own, -100.0, 100.0).astype(jnp.bfloat16)


def draw_values(key, part):
    key = jax.random.fold_in(key, 7)
    shared = periodic(jax.random.fold_in(key, 1), HEADS * DH)
    noise = 0.6 * jax.random.truncated_normal(jax.random.fold_in(key, 2), -5.0, 5.0, (TOKENS, HEADS * DH))
    return (shared + noise).astype(jnp.bfloat16)


def setup_inputs(seed: int = 0, part: int = 0) -> dict:
    key_list = jax.random.split(jax.random.key(seed), 4)
    part_splits = jax.random.split(jax.random.fold_in(key_list[3], part), 4)
    return {
        "queries": draw_queries(jax.random.fold_in(jax.random.fold_in(key_list[3], part), 71), part),
        "keys": draw_keys(jax.random.fold_in(jax.random.fold_in(key_list[3], part), 71), part),
        "values": draw_values(jax.random.fold_in(jax.random.fold_in(key_list[3], part), 71), part),
    }


def coarsen(field, factor):
    rows = field.shape[0] // factor
    return jnp.mean(field.reshape(rows, factor, field.shape[1], field.shape[2]), axis=1)


def pair_terms(query_blocks, key_blocks, value_blocks, weight):
    scale = DH ** -0.5
    scores = jnp.einsum("bihd,bjhd->bhij", query_blocks, key_blocks, precision=lax.Precision.HIGHEST) * scale
    top = jnp.max(scores, axis=-1)
    probs = jnp.exp(scores - top[..., None])
    den = weight * jnp.sum(probs, axis=-1)
    num = weight * jnp.einsum("bhij,bjhd->bihd", probs, value_blocks, precision=lax.Precision.HIGHEST)
    return jnp.swapaxes(top, 1, 2), jnp.swapaxes(den, 1, 2), num


def stretched_terms(query_blocks, key_blocks, value_blocks, weight):
    blocks = query_blocks.shape[0]
    step = min(64, blocks)

    def split(field):
        return field.reshape((blocks // step, step) + field.shape[1:])

    def one(items):
        return pair_terms(items[0], items[1], items[2], weight)

    top, den, num = lax.map(one, (split(query_blocks), split(key_blocks), split(value_blocks)))
    return top.reshape(-1, HEADS), den.reshape(-1, HEADS), num.reshape(-1, HEADS, DH)


def sibling(field):
    supers = field.shape[0] // NB
    paired = field.reshape(supers // 2, 2, NB, HEADS, DH)[:, ::-1]
    return paired.reshape(supers, NB, HEADS, DH)


def expand(field, factor):
    wide = jnp.broadcast_to(field[:, None], (field.shape[0], factor) + field.shape[1:])
    return wide.reshape((field.shape[0] * factor,) + field.shape[1:])


def reference(queries, keys, values):
    total = queries.shape[0]
    q_full = queries.astype(jnp.float32).reshape(total, HEADS, DH)
    k_full = keys.astype(jnp.float32).reshape(total, HEADS, DH)
    v_full = values.astype(jnp.float32).reshape(total, HEADS, DH)
    group = 2 * NB
    shape_near = (total // group, group, HEADS, DH)
    levels = [(1, stretched_terms(q_full.reshape(shape_near), k_full.reshape(shape_near), v_full.reshape(shape_near), 1.0))]
    top_level = (total // NB).bit_length() - 2
    for level in range(1, top_level + 1):
        factor = 2 ** level
        q_coarse = coarsen(q_full, factor)
        k_coarse = coarsen(k_full, factor)
        v_coarse = coarsen(v_full, factor)
        supers = q_coarse.shape[0] // NB
        levels.append((factor, stretched_terms(q_coarse.reshape(supers, NB, HEADS, DH), sibling(k_coarse), sibling(v_coarse), float(factor))))
    largest = None
    for factor, terms in levels:
        spread = expand(terms[0], factor)
        largest = spread if largest is None else jnp.maximum(largest, spread)
    numer = jnp.zeros((total, HEADS, DH), jnp.float32)
    denom = jnp.zeros((total, HEADS), jnp.float32)
    for factor, terms in levels:
        weight = jnp.exp(expand(terms[0], factor) - largest)
        denom = denom + weight * expand(terms[1], factor)
        numer = numer + weight[..., None] * expand(terms[2], factor)
    attended = numer / denom[..., None]
    return attended.reshape(total, HEADS * DH).astype(jnp.bfloat16)
```

```python
import jax
import jax.numpy as jnp
import numpy as np
from jax import lax
from jax.experimental import pallas as pl
from jax.experimental.pallas import tpu as pltpu
from jax.sharding import PartitionSpec as P

HEADS = 2
DH = 128
GROUP = 256
TOKENS_HERE = 512
WIDE = HEADS * DH
SCALE = DH ** (-0.5)
MESH = pl.DeviceIdType.MESH
HIGHEST = lax.Precision.HIGHEST

FIRST = {2: 0, 3: 128, 4: 192, 5: 224, 6: 240, 7: 248, 8: 252}
COARSE = 256
SLOT = 32
PACK = 3 * DH


def reverse(value, bits):
    out = 0
    for _ in range(bits):
        out = out * 2 + value % 2
        value //= 2
    return out


def averaging():
    order = np.zeros((GROUP, GROUP), np.float32)
    for row in range(GROUP):
        order[row, reverse(row, 8)] = 1.0
    near = np.zeros((GROUP // 2, GROUP), np.float32)
    for row in range(GROUP // 2):
        first = reverse(row, 7) * 2
        near[row, first : first + 2] = 0.5
    far = np.zeros((COARSE, TOKENS_HERE), np.float32)
    for level in range(2, 9):
        rows = GROUP >> level
        for group in range(2):
            for row in range(rows):
                first = group * GROUP + (reverse(row, 8 - level) << level)
                far[FIRST[level] + group * rows + row, first : first + (1 << level)] = 0.5**level
    tile = np.zeros((48, SLOT), np.float32)
    for row in range(16):
        tile[row, row] = 1.0
        tile[16 + row, 16 + row // 8 * 4 + row % 4] = 1.0
        tile[32 + row, 24 + row // 8 * 2 + row % 2] = 1.0
    return np.concatenate([order, near]), far, tile


def contract_last(a, b, precision=None):
    return lax.dot_general(
        a, b, (((1,), (1,)), ((), ())), precision=precision, preferred_element_type=jnp.float32
    )


def terms(q, k, v, weight):
    scores = contract_last(q, k, HIGHEST) * SCALE
    top = jnp.max(scores, axis=1, keepdims=True)
    probs = jnp.exp(scores - top)
    den = weight * jnp.sum(probs, axis=1, keepdims=True)
    num = weight * jnp.dot(probs, v, precision=HIGHEST, preferred_element_type=jnp.float32)
    return top, den, num


def merge(a, b):
    top = jnp.maximum(a[0], b[0])
    wa = jnp.exp(a[0] - top)
    wb = jnp.exp(b[0] - top)
    return top, wa * a[1] + wb * b[1], wa * a[2] + wb * b[2]


def double(a):
    return tuple(jnp.concatenate([x, x], axis=0) for x in a)


def head_cols(h):
    return slice(h * DH, (h + 1) * DH)


def pack(parts):
    (top0, den0, num0), (top1, den1, num1) = parts
    rows = num0.shape[0]
    lane = lax.broadcasted_iota(jnp.int32, (rows, DH), 1)
    stats = jnp.where(
        lane < 64, jnp.where(lane < 32, top0, den0), jnp.where(lane < 96, top1, den1)
    )
    return jnp.concatenate([num0, num1, stats], axis=1)


def unpack(x, h):
    at = WIDE + 64 * h
    return x[:, at : at + 1], x[:, at + 32 : at + 33], x[:, head_cols(h)]


def combine(slots):
    out = []
    for h in range(HEADS):
        parts = [unpack(x, h) for x in slots]
        while len(parts) > 1:
            parts = [merge(parts[i], parts[i + 1]) for i in range(0, len(parts), 2)]
        out.append(parts[0])
    return out


def level_of(k):
    return 5 + (k.bit_length() - 1)


def kernel(
    q_hbm, k_hbm, v_hbm, near_hbm, far_hbm, tile_hbm, out_ref,
    q, k, v, near, far, tile,
    kvc, qc, kv2, kv3, kv4, kvz, qg, ret, got, ret8, got8, state,
    load, z_send, z_recv, n_send, n_recv, q_send, q_recv, r_send, r_recv, e_send, e_recv,
):
    me = lax.axis_index("ctx")
    head = lax.axis_index("head")
    z = me // 8

    def peer(mask):
        return (jnp.bitwise_xor(me, mask), head)

    def upper(bit):
        return z // (1 << bit) % 2 == 1

    loads = [
        pltpu.make_async_copy(a, b, load.at[i])
        for i, (a, b) in enumerate(
            [(far_hbm, far), (k_hbm, k), (v_hbm, v), (q_hbm, q), (near_hbm, near), (tile_hbm, tile)]
        )
    ]
    for copy in loads:
        copy.start()

    for m in range(1, 8):
        got8[m * 8 : (m + 1) * 8, :] = jnp.zeros((8, PACK), jnp.float32)

    barrier = pltpu.get_barrier_semaphore()
    for m in range(1, 8):
        pl.semaphore_signal(barrier, inc=1, device_id=peer(m), device_id_type=MESH)
    for bit in range(3, -1, -1):

        @pl.when(jnp.logical_not(upper(bit)))
        def _(bit=bit):
            for j in range(1 << bit, 2 << bit):
                pl.semaphore_signal(barrier, inc=1, device_id=peer(8 * j), device_id_type=MESH)

    def column_copy(j):
        level = level_of(j)
        rows = TOKENS_HERE >> level
        at = (level - 5) * 16 + (j - (1 << (level - 5))) * rows
        return pltpu.make_async_remote_copy(
            kvc.at[pl.ds(FIRST[level], rows)], kvz.at[pl.ds(at, rows)],
            z_send.at[j], z_recv.at[j], device_id=peer(8 * j), device_id_type=MESH,
        )

    def near_copy(i, src, dst, mask):
        return pltpu.make_async_remote_copy(
            src, dst, n_send.at[i], n_recv.at[i], device_id=peer(mask), device_id_type=MESH
        )

    near_copies = [
        near_copy(0, kvc.at[pl.ds(FIRST[2], 128)], kv2, 1),
        near_copy(1, kvc.at[pl.ds(FIRST[3], 64)], kv3.at[pl.ds(0, 64)], 2),
        near_copy(2, kvc.at[pl.ds(FIRST[4], 32)], kv4.at[pl.ds(0, 32)], 4),
        near_copy(3, kvc.at[pl.ds(FIRST[4], 32)], kv4.at[pl.ds(32, 32)], 6),
        near_copy(4, kv3.at[pl.ds(0, 64)], kv3.at[pl.ds(64, 64)], 1),
        near_copy(5, kv4.at[pl.ds(0, 64)], kv4.at[pl.ds(64, 64)], 1),
    ]

    def query_copy(m):
        return pltpu.make_async_remote_copy(
            qg.at[pl.ds(0, SLOT)], qg.at[pl.ds(m * SLOT, SLOT)],
            q_send.at[m], q_recv.at[m], device_id=peer(m), device_id_type=MESH,
        )

    def return_copy(m):
        return pltpu.make_async_remote_copy(
            ret.at[pl.ds(m * SLOT, SLOT)], got.at[pl.ds(m * SLOT, SLOT)],
            r_send.at[m], r_recv.at[m], device_id=peer(m), device_id_type=MESH,
        )

    def last_copy(m):
        return pltpu.make_async_remote_copy(
            ret8.at[pl.ds(m * 8 + 4, 2)], got8.at[pl.ds(m * 8 + 4, 2)],
            e_send.at[m], e_recv.at[m], device_id=peer(m), device_id_type=MESH,
        )

    for copy in loads[:3]:
        copy.wait()
    kvc[:, :WIDE] = jnp.dot(far[...], k[...], preferred_element_type=jnp.float32)
    kvc[:, WIDE:] = jnp.dot(far[...], v[...], preferred_element_type=jnp.float32)

    pl.semaphore_wait(barrier, 7 + z)
    for bit in range(3, -1, -1):

        @pl.when(upper(bit))
        def _(bit=bit):
            for j in range(1 << bit, 2 << bit):
                column_copy(j).start()

    for copy in near_copies[:4]:
        copy.start()
    loads[3].wait()
    qc[...] = jnp.dot(far[...], q[...], preferred_element_type=jnp.float32)
    qg[0:SLOT, :] = qc[FIRST[5] : COARSE, :]
    for m in range(1, 8):
        query_copy(m).start()

    loads[4].wait()
    loads[5].wait()
    ones = jnp.ones((GROUP, DH), jnp.bfloat16)
    q_near, k_near, v_near = [], [], []
    for g in range(2):
        rows = slice(g * GROUP, (g + 1) * GROUP)
        pair = near[GROUP:, :]
        q_near.append(jnp.dot(pair, q[rows, :], preferred_element_type=jnp.float32))
        k_near.append(jnp.dot(pair, k[rows, :], preferred_element_type=jnp.float32))
        v_near.append(jnp.dot(pair, v[rows, :], preferred_element_type=jnp.float32))
    level1 = {}
    for g in range(2):
        rows = slice(g * GROUP, (g + 1) * GROUP)
        ordered = jnp.dot(
            near[:GROUP, :], q[rows, :], preferred_element_type=jnp.float32
        ).astype(jnp.bfloat16)
        for h in range(HEADS):
            cols = head_cols(h)
            scores = contract_last(ordered[:, cols], k[rows, cols]) * SCALE
            top = jnp.max(scores, axis=1, keepdims=True)
            probs = jnp.exp(scores - top)
            high = probs.astype(jnp.bfloat16)
            low = (probs - high.astype(jnp.float32)).astype(jnp.bfloat16)
            wide = jnp.concatenate([v[rows, cols], ones], axis=1)
            both = jnp.dot(high, wide, preferred_element_type=jnp.float32) + jnp.dot(
                low, wide, preferred_element_type=jnp.float32
            )
            state[g, h, 0] = jnp.broadcast_to(top, (GROUP, DH))
            state[g, h, 1] = both[:, DH:]
            state[g, h, 2] = both[:, :DH]
            level1[g, h] = terms(
                q_near[g][:, cols], k_near[1 - g][:, cols], v_near[1 - g][:, cols], 2.0
            )

    near_copies[1].wait_recv()
    near_copies[4].start()
    near_copies[2].wait_recv()
    near_copies[3].wait_recv()
    near_copies[5].start()

    near_copies[0].wait_recv()
    level2 = [
        terms(qc[0:128, head_cols(h)], kv2[:, head_cols(h)], kv2[:, head_cols(h + 2)], 4.0)
        for h in range(HEADS)
    ]
    near_copies[4].wait_recv()
    level3 = [
        terms(qc[128:192, head_cols(h)], kv3[:, head_cols(h)], kv3[:, head_cols(h + 2)], 8.0)
        for h in range(HEADS)
    ]
    near_copies[5].wait_recv()
    level4 = [
        terms(qc[192:224, head_cols(h)], kv4[:, head_cols(h)], kv4[:, head_cols(h + 2)], 16.0)
        for h in range(HEADS)
    ]
    for g in range(2):
        for h in range(HEADS):
            joined = tuple(x[g * 16 : (g + 1) * 16] for x in level4[h])
            joined = merge(tuple(x[g * 32 : (g + 1) * 32] for x in level3[h]), double(joined))
            joined = merge(tuple(x[g * 64 : (g + 1) * 64] for x in level2[h]), double(joined))
            joined = double(merge(level1[g, h], double(joined)))
            top, den, num = merge((state[g, h, 0], state[g, h, 1], state[g, h, 2]), joined)
            state[g, h, 0] = top
            state[g, h, 1] = den
            state[g, h, 2] = num

    def take(bit):
        for j in range((2 << bit) - 1, (1 << bit) - 1, -1):
            column_copy(j).wait_recv()

            @pl.when(jnp.logical_not(upper(bit)))
            def _(j=j):
                column_copy(j).start()

    def partial(level, queries):
        at = (level - 5) * 16
        return pack(
            [
                terms(
                    queries[:, head_cols(h)],
                    kvz[at : at + 16, head_cols(h)],
                    kvz[at : at + 16, head_cols(h + 2)],
                    float(2**level),
                )
                for h in range(HEADS)
            ]
        )

    def queries_of(first, rows):
        return jnp.concatenate(
            [qg[m * SLOT + first : m * SLOT + first + rows, :] for m in range(8)], axis=0
        )

    for m in range(1, 8):
        query_copy(m).wait_recv()
    for bit, first, rows in ((0, 0, 16), (1, 16, 8), (2, 24, 8)):
        take(bit)
        result = partial(5 + bit, queries_of(first, rows))
        for m in range(8):
            ret[m * SLOT + first : m * SLOT + first + rows, :] = result[m * rows : (m + 1) * rows]
    for m in range(1, 8):
        return_copy(m).start()
    for m in range(1, 8):
        return_copy(m).wait_recv()
    parts = combine([ret[0:SLOT, :]] + [got[m * SLOT : (m + 1) * SLOT, :] for m in range(1, 8)])
    spread = jnp.dot(tile[...], pack(parts), precision=HIGHEST, preferred_element_type=jnp.float32)
    for g in range(2):
        for h in range(HEADS):
            five, six, seven = (
                unpack(spread[16 * i + 8 * g : 16 * i + 8 * g + 8, :], h) for i in range(3)
            )
            joined = merge(five, merge(six, seven))
            for _ in range(5):
                joined = double(joined)
            top, den, num = merge((state[g, h, 0], state[g, h, 1], state[g, h, 2]), joined)
            state[g, h, 0] = top
            state[g, h, 1] = den
            state[g, h, 2] = num

    queries = queries_of(24, 8)
    take(3)
    ret8[...] = partial(8, queries)
    for m in range(1, 8):
        last_copy(m).start()
    for m in range(1, 8):
        last_copy(m).wait_recv()
    parts = combine([ret8[0:8, :]] + [got8[m * 8 : (m + 1) * 8, :] for m in range(1, 8)])
    for g in range(2):
        attended = []
        for h in range(HEADS):
            row = tuple(x[4 + g : 5 + g, :] for x in parts[h])
            top = jnp.maximum(state[g, h, 0], row[0])
            wa = jnp.exp(state[g, h, 0] - top)
            wb = jnp.exp(row[0] - top)
            den = wa * state[g, h, 1] + wb * row[1]
            num = wa * state[g, h, 2] + wb * row[2]
            attended.append((num / den).astype(jnp.bfloat16))
        out_ref[g * GROUP : (g + 1) * GROUP, :] = jnp.dot(
            near[:GROUP, :], jnp.concatenate(attended, axis=1), preferred_element_type=jnp.float32
        ).astype(jnp.bfloat16)

    for j in range(1, 16):
        column_copy(j).wait_send()
    for copy in near_copies:
        copy.wait_send()
    for m in range(1, 8):
        query_copy(m).wait_send()
        return_copy(m).wait_send()
        last_copy(m).wait_send()


def on_device(queries, keys, values):
    near, far, tile = averaging()
    near = jnp.asarray(near, jnp.bfloat16)
    far = jnp.asarray(far, jnp.bfloat16)
    tile = jnp.asarray(tile, jnp.float32)
    f32, bf16 = jnp.float32, jnp.bfloat16
    whole = (TOKENS_HERE, WIDE)
    dma = pltpu.SemaphoreType.DMA
    return pl.pallas_call(
        kernel,
        out_shape=jax.ShapeDtypeStruct(whole, bf16),
        in_specs=[pl.BlockSpec(memory_space=pl.ANY)] * 6,
        out_specs=pl.BlockSpec(memory_space=pltpu.VMEM),
        scratch_shapes=[
            pltpu.VMEM(whole, bf16),
            pltpu.VMEM(whole, bf16),
            pltpu.VMEM(whole, bf16),
            pltpu.VMEM(near.shape, bf16),
            pltpu.VMEM(far.shape, bf16),
            pltpu.VMEM(tile.shape, f32),
            pltpu.VMEM((COARSE, 2 * WIDE), f32),
            pltpu.VMEM((COARSE, WIDE), f32),
            pltpu.VMEM((128, 2 * WIDE), f32),
            pltpu.VMEM((128, 2 * WIDE), f32),
            pltpu.VMEM((128, 2 * WIDE), f32),
            pltpu.VMEM((64, 2 * WIDE), f32),
            pltpu.VMEM((8 * SLOT, WIDE), f32),
            pltpu.VMEM((8 * SLOT, PACK), f32),
            pltpu.VMEM((8 * SLOT, PACK), f32),
            pltpu.VMEM((64, PACK), f32),
            pltpu.VMEM((64, PACK), f32),
            pltpu.VMEM((2, HEADS, 3, GROUP, DH), f32),
            dma((6,)),
            dma((16,)),
            dma((16,)),
            dma((6,)),
            dma((6,)),
            dma((8,)),
            dma((8,)),
            dma((8,)),
            dma((8,)),
            dma((8,)),
            dma((8,)),
        ],
        compiler_params=pltpu.CompilerParams(
            collective_id=0, has_side_effects=True, vmem_limit_bytes=48 * 2**20
        ),
    )(queries, keys, values, near, far, tile)


def solution(mesh):
    in_specs = (P("ctx", "head"), P("ctx", "head"), P("ctx", "head"))
    return jax.shard_map(
        on_device, mesh=mesh, in_specs=in_specs, out_specs=P("ctx", "head"), check_vma=False
    )
```

```python
import jax
import jax.numpy as jnp
import numpy as np
from jax import lax
from jax.experimental import pallas as pl
from jax.experimental.pallas import tpu as pltpu
from jax.sharding import PartitionSpec as P

HEADS = 2
DH = 128
GROUP = 256
TOKENS_HERE = 512
WIDE = HEADS * DH
SCALE = DH ** (-0.5)
MESH = pl.DeviceIdType.MESH
HIGHEST = lax.Precision.HIGHEST

FIRST = {2: 0, 3: 128, 4: 192, 5: 224, 6: 240, 7: 248, 8: 252}
COARSE = 256
SLOT = 32
PACK = 3 * DH


def reverse(value, bits):
    out = 0
    for _ in range(bits):
        out = out * 2 + value % 2
        value //= 2
    return out


def averaging():
    order = np.zeros((GROUP, GROUP), np.float32)
    for row in range(GROUP):
        order[row, reverse(row, 8)] = 1.0
    near = np.zeros((GROUP // 2, GROUP), np.float32)
    for row in range(GROUP // 2):
        first = reverse(row, 7) * 2
        near[row, first : first + 2] = 0.5
    far = np.zeros((COARSE, TOKENS_HERE), np.float32)
    for level in range(2, 9):
        rows = GROUP >> level
        for group in range(2):
            for row in range(rows):
                first = group * GROUP + (reverse(row, 8 - level) << level)
                far[FIRST[level] + group * rows + row, first : first + (1 << level)] = 0.5**level
    tile = np.zeros((48, SLOT), np.float32)
    for row in range(16):
        tile[row, row] = 1.0
        tile[16 + row, 16 + row // 8 * 4 + row % 4] = 1.0
        tile[32 + row, 24 + row // 8 * 2 + row % 2] = 1.0
    return np.concatenate([order, near]), far, tile


def contract_last(a, b, precision=None):
    return lax.dot_general(
        a, b, (((1,), (1,)), ((), ())), precision=precision, preferred_element_type=jnp.float32
    )


def terms(q, k, v, weight):
    scores = contract_last(q, k, HIGHEST) * SCALE
    top = jnp.max(scores, axis=1, keepdims=True)
    probs = jnp.exp(scores - top)
    den = weight * jnp.sum(probs, axis=1, keepdims=True)
    num = weight * jnp.dot(probs, v, precision=HIGHEST, preferred_element_type=jnp.float32)
    return top, den, num


def merge(a, b):
    top = jnp.maximum(a[0], b[0])
    wa = jnp.exp(a[0] - top)
    wb = jnp.exp(b[0] - top)
    return top, wa * a[1] + wb * b[1], wa * a[2] + wb * b[2]


def double(a):
    return tuple(jnp.concatenate([x, x], axis=0) for x in a)


def head_cols(h):
    return slice(h * DH, (h + 1) * DH)


def pack(parts):
    (top0, den0, num0), (top1, den1, num1) = parts
    rows = num0.shape[0]
    lane = lax.broadcasted_iota(jnp.int32, (rows, DH), 1)
    stats = jnp.where(
        lane < 64, jnp.where(lane < 32, top0, den0), jnp.where(lane < 96, top1, den1)
    )
    return jnp.concatenate([num0, num1, stats], axis=1)


def unpack(x, h):
    at = WIDE + 64 * h
    return x[:, at : at + 1], x[:, at + 32 : at + 33], x[:, head_cols(h)]


def combine(slots):
    out = []
    for h in range(HEADS):
        parts = [unpack(x, h) for x in slots]
        while len(parts) > 1:
            parts = [merge(parts[i], parts[i + 1]) for i in range(0, len(parts), 2)]
        out.append(parts[0])
    return out


def level_of(k):
    return 5 + (k.bit_length() - 1)


def kernel(
    q_hbm, k_hbm, v_hbm, near_hbm, far_hbm, tile_hbm, out_ref,
    q, k, v, near, far, tile,
    kvc, qc, kv2, kv3, kv4, kvz, kvo, qg, q8, ret, got, ret8, got8, state,
    load, z_send, z_recv, n_send, n_recv, q_send, q_recv, r_send, r_recv, e_send, e_recv,
):
    me = lax.axis_index("ctx")
    head = lax.axis_index("head")
    z = me // 8

    def peer(mask):
        return (jnp.bitwise_xor(me, mask), head)

    def upper(bit):
        return z // (1 << bit) % 2 == 1

    loads = [
        pltpu.make_async_copy(a, b, load.at[i])
        for i, (a, b) in enumerate(
            [(far_hbm, far), (k_hbm, k), (v_hbm, v), (q_hbm, q), (near_hbm, near), (tile_hbm, tile)]
        )
    ]
    for copy in loads:
        copy.start()

    for m in range(1, 8):
        got8[m * 8 : (m + 1) * 8, :] = jnp.zeros((8, PACK), jnp.float32)

    barrier = pltpu.get_barrier_semaphore()
    for m in range(1, 8):
        pl.semaphore_signal(barrier, inc=1, device_id=peer(m), device_id_type=MESH)
    for bit in range(3, -1, -1):

        @pl.when(jnp.logical_not(upper(bit)))
        def _(bit=bit):
            for j in range(1 << bit, 2 << bit):
                pl.semaphore_signal(barrier, inc=1, device_id=peer(8 * j), device_id_type=MESH)

    def column_copy(j):
        level = level_of(j)
        rows = TOKENS_HERE >> level
        at = (level - 5) * 16 + (j - (1 << (level - 5))) * rows
        return pltpu.make_async_remote_copy(
            kvc.at[pl.ds(FIRST[level], rows)], kvz.at[pl.ds(at, rows)],
            z_send.at[j], z_recv.at[j], device_id=peer(8 * j), device_id_type=MESH,
        )

    def near_copy(i, src, dst, mask):
        return pltpu.make_async_remote_copy(
            src, dst, n_send.at[i], n_recv.at[i], device_id=peer(mask), device_id_type=MESH
        )

    near_copies = [
        near_copy(0, kvc.at[pl.ds(FIRST[2], 128)], kv2, 1),
        near_copy(1, kvc.at[pl.ds(FIRST[3], 64)], kv3.at[pl.ds(0, 64)], 2),
        near_copy(2, kvc.at[pl.ds(FIRST[4], 32)], kv4.at[pl.ds(0, 32)], 4),
        near_copy(3, kvc.at[pl.ds(FIRST[4], 32)], kv4.at[pl.ds(32, 32)], 6),
        near_copy(4, kv3.at[pl.ds(0, 64)], kv3.at[pl.ds(64, 64)], 1),
        near_copy(5, kv4.at[pl.ds(0, 64)], kv4.at[pl.ds(64, 64)], 1),
        near_copy(6, kvz.at[pl.ds(0, 48)], kvo, 1),
    ]

    def query_copy(m):
        if m % 2 == 0:
            src, dst = qg.at[pl.ds(0, SLOT)], qg.at[pl.ds(m // 2 * SLOT, SLOT)]
        else:
            src, dst = qg.at[pl.ds(24, 8)], q8.at[pl.ds(m // 2 * 8, 8)]
        return pltpu.make_async_remote_copy(
            src, dst, q_send.at[m], q_recv.at[m], device_id=peer(m), device_id_type=MESH
        )

    def return_copy(m):
        rows = pl.ds(m // 2 * SLOT, SLOT)
        return pltpu.make_async_remote_copy(
            ret.at[rows], got.at[rows],
            r_send.at[m], r_recv.at[m], device_id=peer(m), device_id_type=MESH,
        )

    def last_copy(m):
        return pltpu.make_async_remote_copy(
            ret8.at[pl.ds(m * 8 + 4, 2)], got8.at[pl.ds(m * 8 + 4, 2)],
            e_send.at[m], e_recv.at[m], device_id=peer(m), device_id_type=MESH,
        )

    for copy in loads[:3]:
        copy.wait()
    kvc[:, :WIDE] = jnp.dot(far[...], k[...], preferred_element_type=jnp.float32)
    kvc[:, WIDE:] = jnp.dot(far[...], v[...], preferred_element_type=jnp.float32)

    pl.semaphore_wait(barrier, 7 + z)
    for bit in range(3, -1, -1):

        @pl.when(upper(bit))
        def _(bit=bit):
            for j in range(1 << bit, 2 << bit):
                column_copy(j).start()

    for copy in near_copies[:4]:
        copy.start()
    loads[3].wait()
    qc[...] = jnp.dot(far[...], q[...], preferred_element_type=jnp.float32)
    qg[0:SLOT, :] = qc[FIRST[5] : COARSE, :]
    for m in range(1, 8):
        query_copy(m).start()

    loads[4].wait()
    loads[5].wait()
    ones = jnp.ones((GROUP, DH), jnp.bfloat16)
    q_near, k_near, v_near = [], [], []
    for g in range(2):
        rows = slice(g * GROUP, (g + 1) * GROUP)
        pair = near[GROUP:, :]
        q_near.append(jnp.dot(pair, q[rows, :], preferred_element_type=jnp.float32))
        k_near.append(jnp.dot(pair, k[rows, :], preferred_element_type=jnp.float32))
        v_near.append(jnp.dot(pair, v[rows, :], preferred_element_type=jnp.float32))
    level1 = {}
    for g in range(2):
        rows = slice(g * GROUP, (g + 1) * GROUP)
        ordered = jnp.dot(
            near[:GROUP, :], q[rows, :], preferred_element_type=jnp.float32
        ).astype(jnp.bfloat16)
        for h in range(HEADS):
            cols = head_cols(h)
            scores = contract_last(ordered[:, cols], k[rows, cols]) * SCALE
            top = jnp.max(scores, axis=1, keepdims=True)
            probs = jnp.exp(scores - top)
            high = probs.astype(jnp.bfloat16)
            low = (probs - high.astype(jnp.float32)).astype(jnp.bfloat16)
            wide = jnp.concatenate([v[rows, cols], ones], axis=1)
            both = jnp.dot(high, wide, preferred_element_type=jnp.float32) + jnp.dot(
                low, wide, preferred_element_type=jnp.float32
            )
            state[g, h, 0] = jnp.broadcast_to(top, (GROUP, DH))
            state[g, h, 1] = both[:, DH:]
            state[g, h, 2] = both[:, :DH]
            level1[g, h] = terms(
                q_near[g][:, cols], k_near[1 - g][:, cols], v_near[1 - g][:, cols], 2.0
            )

    def answer(bit, here):
        @pl.when(jnp.logical_and(here, jnp.logical_not(upper(bit))))
        def _():
            for j in range((2 << bit) - 1, (1 << bit) - 1, -1):
                column_copy(j).wait_recv()
                column_copy(j).start()

    for bit in range(3):
        answer(bit, z >= 3)
    near_copies[1].wait_recv()
    near_copies[4].start()
    near_copies[2].wait_recv()
    near_copies[3].wait_recv()
    near_copies[5].start()

    near_copies[0].wait_recv()
    level2 = [
        terms(qc[0:128, head_cols(h)], kv2[:, head_cols(h)], kv2[:, head_cols(h + 2)], 4.0)
        for h in range(HEADS)
    ]
    near_copies[4].wait_recv()
    level3 = [
        terms(qc[128:192, head_cols(h)], kv3[:, head_cols(h)], kv3[:, head_cols(h + 2)], 8.0)
        for h in range(HEADS)
    ]
    near_copies[5].wait_recv()
    level4 = [
        terms(qc[192:224, head_cols(h)], kv4[:, head_cols(h)], kv4[:, head_cols(h + 2)], 16.0)
        for h in range(HEADS)
    ]
    answer(3, z >= 3)
    for g in range(2):
        for h in range(HEADS):
            joined = tuple(x[g * 16 : (g + 1) * 16] for x in level4[h])
            joined = merge(tuple(x[g * 32 : (g + 1) * 32] for x in level3[h]), double(joined))
            joined = merge(tuple(x[g * 64 : (g + 1) * 64] for x in level2[h]), double(joined))
            joined = double(merge(level1[g, h], double(joined)))
            top, den, num = merge((state[g, h, 0], state[g, h, 1], state[g, h, 2]), joined)
            state[g, h, 0] = top
            state[g, h, 1] = den
            state[g, h, 2] = num

    def collect(bit):
        @pl.when(upper(bit))
        def _():
            for j in range((2 << bit) - 1, (1 << bit) - 1, -1):
                column_copy(j).wait_recv()

    def partial(level, queries, fields):
        return pack(
            [
                terms(
                    queries[:, head_cols(h)],
                    fields[:, head_cols(h)],
                    fields[:, head_cols(h + 2)],
                    float(2**level),
                )
                for h in range(HEADS)
            ]
        )

    for bit in range(3):
        answer(bit, z < 3)
        collect(bit)
    near_copies[6].start()
    for m in range(1, 8):
        query_copy(m).wait_recv()
    near_copies[6].wait_recv()
    for bit, first, rows in ((0, 0, 16), (1, 16, 8), (2, 24, 8)):
        queries = jnp.concatenate(
            [qg[i * SLOT + first : i * SLOT + first + rows, :] for i in range(4)], axis=0
        )
        fields = jnp.concatenate(
            [kvz[16 * bit : 16 * bit + 16, :], kvo[16 * bit : 16 * bit + 16, :]], axis=0
        )
        result = partial(5 + bit, queries, fields)
        for i in range(4):
            ret[i * SLOT + first : i * SLOT + first + rows, :] = result[i * rows : (i + 1) * rows]
    for m in (2, 4, 6):
        return_copy(m).start()
    answer(3, z < 3)
    collect(3)
    queries = []
    for m in range(8):
        queries.append(
            q8[m // 2 * 8 : m // 2 * 8 + 8, :]
            if m % 2
            else qg[m // 2 * SLOT + 24 : (m // 2 + 1) * SLOT, :]
        )
    ret8[...] = partial(8, jnp.concatenate(queries, axis=0), kvz[48:64, :])
    for m in range(1, 8):
        last_copy(m).start()
    for m in (2, 4, 6):
        return_copy(m).wait_recv()
    parts = combine([ret[0:SLOT, :]] + [got[i * SLOT : (i + 1) * SLOT, :] for i in range(1, 4)])
    spread = jnp.dot(tile[...], pack(parts), precision=HIGHEST, preferred_element_type=jnp.float32)
    for g in range(2):
        for h in range(HEADS):
            five, six, seven = (
                unpack(spread[16 * i + 8 * g : 16 * i + 8 * g + 8, :], h) for i in range(3)
            )
            joined = merge(five, merge(six, seven))
            for _ in range(5):
                joined = double(joined)
            top, den, num = merge((state[g, h, 0], state[g, h, 1], state[g, h, 2]), joined)
            state[g, h, 0] = top
            state[g, h, 1] = den
            state[g, h, 2] = num
    for m in range(1, 8):
        last_copy(m).wait_recv()
    parts = combine([ret8[0:8, :]] + [got8[m * 8 : (m + 1) * 8, :] for m in range(1, 8)])
    for g in range(2):
        attended = []
        for h in range(HEADS):
            row = tuple(x[4 + g : 5 + g, :] for x in parts[h])
            top = jnp.maximum(state[g, h, 0], row[0])
            wa = jnp.exp(state[g, h, 0] - top)
            wb = jnp.exp(row[0] - top)
            den = wa * state[g, h, 1] + wb * row[1]
            num = wa * state[g, h, 2] + wb * row[2]
            attended.append((num / den).astype(jnp.bfloat16))
        out_ref[g * GROUP : (g + 1) * GROUP, :] = jnp.dot(
            near[:GROUP, :], jnp.concatenate(attended, axis=1), preferred_element_type=jnp.float32
        ).astype(jnp.bfloat16)

    for j in range(1, 16):
        column_copy(j).wait_send()
    for copy in near_copies:
        copy.wait_send()
    for m in range(1, 8):
        query_copy(m).wait_send()
        last_copy(m).wait_send()
    for m in (2, 4, 6):
        return_copy(m).wait_send()


def on_device(queries, keys, values):
    near, far, tile = averaging()
    near = jnp.asarray(near, jnp.bfloat16)
    far = jnp.asarray(far, jnp.bfloat16)
    tile = jnp.asarray(tile, jnp.float32)
    f32, bf16 = jnp.float32, jnp.bfloat16
    whole = (TOKENS_HERE, WIDE)
    dma = pltpu.SemaphoreType.DMA
    return pl.pallas_call(
        kernel,
        out_shape=jax.ShapeDtypeStruct(whole, bf16),
        in_specs=[pl.BlockSpec(memory_space=pl.ANY)] * 6,
        out_specs=pl.BlockSpec(memory_space=pltpu.VMEM),
        scratch_shapes=[
            pltpu.VMEM(whole, bf16),
            pltpu.VMEM(whole, bf16),
            pltpu.VMEM(whole, bf16),
            pltpu.VMEM(near.shape, bf16),
            pltpu.VMEM(far.shape, bf16),
            pltpu.VMEM(tile.shape, f32),
            pltpu.VMEM((COARSE, 2 * WIDE), f32),
            pltpu.VMEM((COARSE, WIDE), f32),
            pltpu.VMEM((128, 2 * WIDE), f32),
            pltpu.VMEM((128, 2 * WIDE), f32),
            pltpu.VMEM((128, 2 * WIDE), f32),
            pltpu.VMEM((64, 2 * WIDE), f32),
            pltpu.VMEM((48, 2 * WIDE), f32),
            pltpu.VMEM((4 * SLOT, WIDE), f32),
            pltpu.VMEM((32, WIDE), f32),
            pltpu.VMEM((4 * SLOT, PACK), f32),
            pltpu.VMEM((4 * SLOT, PACK), f32),
            pltpu.VMEM((64, PACK), f32),
            pltpu.VMEM((64, PACK), f32),
            pltpu.VMEM((2, HEADS, 3, GROUP, DH), f32),
            dma((6,)),
            dma((16,)),
            dma((16,)),
            dma((7,)),
            dma((7,)),
            dma((8,)),
            dma((8,)),
            dma((8,)),
            dma((8,)),
            dma((8,)),
            dma((8,)),
        ],
        compiler_params=pltpu.CompilerParams(
            collective_id=0, has_side_effects=True, vmem_limit_bytes=48 * 2**20
        ),
    )(queries, keys, values, near, far, tile)


def solution(mesh):
    in_specs = (P("ctx", "head"), P("ctx", "head"), P("ctx", "head"))
    return jax.shard_map(
        on_device, mesh=mesh, in_specs=in_specs, out_specs=P("ctx", "head"), check_vma=False
    )
```

```python
import jax
import jax.numpy as jnp
import numpy as np
from jax import lax
from jax.experimental import pallas as pl
from jax.experimental.pallas import tpu as pltpu
from jax.sharding import PartitionSpec as P

HEADS = 2
DH = 128
GROUP = 256
TOKENS_HERE = 512
WIDE = HEADS * DH
SCALE = DH ** (-0.5)
MESH = pl.DeviceIdType.MESH
HIGHEST = lax.Precision.HIGHEST

FIRST = {2: 0, 3: 128, 4: 192, 5: 224, 6: 240, 7: 248, 8: 252}
COARSE = 256
SLOT = 32
PACK = 3 * DH


def reverse(value, bits):
    out = 0
    for _ in range(bits):
        out = out * 2 + value % 2
        value //= 2
    return out


def averaging():
    order = np.zeros((GROUP, GROUP), np.float32)
    for row in range(GROUP):
        order[row, reverse(row, 8)] = 1.0
    near = np.zeros((GROUP // 2, GROUP), np.float32)
    for row in range(GROUP // 2):
        first = reverse(row, 7) * 2
        near[row, first : first + 2] = 0.5
    far = np.zeros((COARSE, TOKENS_HERE), np.float32)
    for level in range(2, 9):
        rows = GROUP >> level
        for group in range(2):
            for row in range(rows):
                first = group * GROUP + (reverse(row, 8 - level) << level)
                far[FIRST[level] + group * rows + row, first : first + (1 << level)] = 0.5**level
    tile = np.zeros((48, SLOT), np.float32)
    for row in range(16):
        tile[row, row] = 1.0
        tile[16 + row, 16 + row // 8 * 4 + row % 4] = 1.0
        tile[32 + row, 24 + row // 8 * 2 + row % 2] = 1.0
    return np.concatenate([order, near]), far, tile


def contract_last(a, b, precision=None):
    return lax.dot_general(
        a, b, (((1,), (1,)), ((), ())), precision=precision, preferred_element_type=jnp.float32
    )


def halves(x):
    high = x.astype(jnp.bfloat16)
    return high, (x - high.astype(jnp.float32)).astype(jnp.bfloat16)


def terms(q, k, v, weight):
    keys = k.shape[0]
    q_both = jnp.concatenate(halves(q * SCALE), axis=1)
    k_high, k_low = halves(k)
    k_high = jnp.concatenate([k_high, k_high], axis=1)
    k_low = jnp.concatenate([k_low, k_low], axis=1)
    v_both = jnp.concatenate(halves(v), axis=1)
    if keys == DH:
        scores = contract_last(q_both, jnp.concatenate([k_high, k_low], axis=0))
        scores = scores[:, :DH] + scores[:, DH:]
    else:
        scores = contract_last(q_both, k_high) + contract_last(q_both, k_low)
    top = jnp.max(scores, axis=1, keepdims=True)
    probs = jnp.exp(scores - top)
    den = weight * jnp.sum(probs, axis=1, keepdims=True)
    p_high, p_low = halves(probs * weight)
    if keys == DH:
        p_both = jnp.concatenate([p_high, p_low], axis=1)
        num = jnp.dot(
            p_both,
            jnp.concatenate([v_both, v_both], axis=0),
            preferred_element_type=jnp.float32,
        )
    else:
        num = jnp.dot(p_high, v_both, preferred_element_type=jnp.float32) + jnp.dot(
            p_low, v_both, preferred_element_type=jnp.float32
        )
    return top, den, num[:, :DH] + num[:, DH:]


def merge(a, b):
    top = jnp.maximum(a[0], b[0])
    wa = jnp.exp(a[0] - top)
    wb = jnp.exp(b[0] - top)
    return top, wa * a[1] + wb * b[1], wa * a[2] + wb * b[2]


def double(a):
    return tuple(jnp.concatenate([x, x], axis=0) for x in a)


def head_cols(h):
    return slice(h * DH, (h + 1) * DH)


def pack(parts):
    (top0, den0, num0), (top1, den1, num1) = parts
    rows = num0.shape[0]
    lane = lax.broadcasted_iota(jnp.int32, (rows, DH), 1)
    stats = jnp.where(
        lane < 64, jnp.where(lane < 32, top0, den0), jnp.where(lane < 96, top1, den1)
    )
    return jnp.concatenate([num0, num1, stats], axis=1)


def unpack(x, h):
    at = WIDE + 64 * h
    return x[:, at : at + 1], x[:, at + 32 : at + 33], x[:, head_cols(h)]


def combine(slots):
    out = []
    for h in range(HEADS):
        parts = [unpack(x, h) for x in slots]
        while len(parts) > 1:
            parts = [merge(parts[i], parts[i + 1]) for i in range(0, len(parts), 2)]
        out.append(parts[0])
    return out


def level_of(k):
    return 5 + (k.bit_length() - 1)


def kernel(
    q_hbm, k_hbm, v_hbm, near_hbm, far_hbm, tile_hbm, out_ref,
    q, k, v, near, far, tile,
    kvc, qc, kv2, kv3, kv4, kvz, kvo, qg, q8, ret, got, ret8, got8, state,
    load, z_send, z_recv, n_send, n_recv, q_send, q_recv, r_send, r_recv, e_send, e_recv,
):
    me = lax.axis_index("ctx")
    head = lax.axis_index("head")
    z = me // 8

    def peer(mask):
        return (jnp.bitwise_xor(me, mask), head)

    def upper(bit):
        return z // (1 << bit) % 2 == 1

    loads = [
        pltpu.make_async_copy(a, b, load.at[i])
        for i, (a, b) in enumerate(
            [(far_hbm, far), (k_hbm, k), (v_hbm, v), (q_hbm, q), (near_hbm, near), (tile_hbm, tile)]
        )
    ]
    for copy in loads:
        copy.start()

    for m in range(1, 8):
        got8[m * 8 : (m + 1) * 8, :] = jnp.zeros((8, PACK), jnp.float32)

    barrier = pltpu.get_barrier_semaphore()
    for m in range(1, 8):
        pl.semaphore_signal(barrier, inc=1, device_id=peer(m), device_id_type=MESH)
    for bit in range(3, -1, -1):

        @pl.when(jnp.logical_not(upper(bit)))
        def _(bit=bit):
            for j in range(1 << bit, 2 << bit):
                pl.semaphore_signal(barrier, inc=1, device_id=peer(8 * j), device_id_type=MESH)

    def column_copy(j):
        level = level_of(j)
        rows = TOKENS_HERE >> level
        at = (level - 5) * 16 + (j - (1 << (level - 5))) * rows
        return pltpu.make_async_remote_copy(
            kvc.at[pl.ds(FIRST[level], rows)], kvz.at[pl.ds(at, rows)],
            z_send.at[j], z_recv.at[j], device_id=peer(8 * j), device_id_type=MESH,
        )

    def near_copy(i, src, dst, mask):
        return pltpu.make_async_remote_copy(
            src, dst, n_send.at[i], n_recv.at[i], device_id=peer(mask), device_id_type=MESH
        )

    near_copies = [
        near_copy(0, kvc.at[pl.ds(FIRST[2], 128)], kv2, 1),
        near_copy(1, kvc.at[pl.ds(FIRST[3], 64)], kv3.at[pl.ds(0, 64)], 2),
        near_copy(2, kvc.at[pl.ds(FIRST[4], 32)], kv4.at[pl.ds(0, 32)], 4),
        near_copy(3, kvc.at[pl.ds(FIRST[4], 32)], kv4.at[pl.ds(32, 32)], 6),
        near_copy(4, kv3.at[pl.ds(0, 64)], kv3.at[pl.ds(64, 64)], 1),
        near_copy(5, kv4.at[pl.ds(0, 64)], kv4.at[pl.ds(64, 64)], 1),
        near_copy(6, kvz.at[pl.ds(0, 48)], kvo, 1),
    ]

    def query_copy(m):
        if m % 2 == 0:
            src, dst = qg.at[pl.ds(0, SLOT)], qg.at[pl.ds(m // 2 * SLOT, SLOT)]
        else:
            src, dst = qg.at[pl.ds(24, 8)], q8.at[pl.ds(m // 2 * 8, 8)]
        return pltpu.make_async_remote_copy(
            src, dst, q_send.at[m], q_recv.at[m], device_id=peer(m), device_id_type=MESH
        )

    def return_copy(m):
        rows = pl.ds(m // 2 * SLOT, SLOT)
        return pltpu.make_async_remote_copy(
            ret.at[rows], got.at[rows],
            r_send.at[m], r_recv.at[m], device_id=peer(m), device_id_type=MESH,
        )

    def last_copy(m):
        return pltpu.make_async_remote_copy(
            ret8.at[pl.ds(m * 8 + 4, 2)], got8.at[pl.ds(m * 8 + 4, 2)],
            e_send.at[m], e_recv.at[m], device_id=peer(m), device_id_type=MESH,
        )

    for copy in loads[:3]:
        copy.wait()
    kvc[:, :WIDE] = jnp.dot(far[...], k[...], preferred_element_type=jnp.float32)
    kvc[:, WIDE:] = jnp.dot(far[...], v[...], preferred_element_type=jnp.float32)

    pl.semaphore_wait(barrier, 7 + z)
    for bit in range(3, -1, -1):

        @pl.when(upper(bit))
        def _(bit=bit):
            for j in range(1 << bit, 2 << bit):
                column_copy(j).start()

    for copy in near_copies[:4]:
        copy.start()
    loads[3].wait()
    qc[...] = jnp.dot(far[...], q[...], preferred_element_type=jnp.float32)
    qg[0:SLOT, :] = qc[FIRST[5] : COARSE, :]
    for m in range(1, 8):
        query_copy(m).start()

    loads[4].wait()
    loads[5].wait()
    ones = jnp.ones((GROUP, DH), jnp.bfloat16)
    q_near, k_near, v_near = [], [], []
    for g in range(2):
        rows = slice(g * GROUP, (g + 1) * GROUP)
        pair = near[GROUP:, :]
        q_near.append(jnp.dot(pair, q[rows, :], preferred_element_type=jnp.float32))
        k_near.append(jnp.dot(pair, k[rows, :], preferred_element_type=jnp.float32))
        v_near.append(jnp.dot(pair, v[rows, :], preferred_element_type=jnp.float32))
    level1 = {}
    for g in range(2):
        rows = slice(g * GROUP, (g + 1) * GROUP)
        ordered = jnp.dot(
            near[:GROUP, :], q[rows, :], preferred_element_type=jnp.float32
        ).astype(jnp.bfloat16)
        for h in range(HEADS):
            cols = head_cols(h)
            scores = contract_last(ordered[:, cols], k[rows, cols]) * SCALE
            top = jnp.max(scores, axis=1, keepdims=True)
            probs = jnp.exp(scores - top)
            high = probs.astype(jnp.bfloat16)
            low = (probs - high.astype(jnp.float32)).astype(jnp.bfloat16)
            wide = jnp.concatenate([v[rows, cols], ones], axis=1)
            both = jnp.dot(high, wide, preferred_element_type=jnp.float32) + jnp.dot(
                low, wide, preferred_element_type=jnp.float32
            )
            state[g, h, 0] = jnp.broadcast_to(top, (GROUP, DH))
            state[g, h, 1] = both[:, DH:]
            state[g, h, 2] = both[:, :DH]
            level1[g, h] = terms(
                q_near[g][:, cols], k_near[1 - g][:, cols], v_near[1 - g][:, cols], 2.0
            )

    def answer(bit, here):
        @pl.when(jnp.logical_and(here, jnp.logical_not(upper(bit))))
        def _():
            for j in range((2 << bit) - 1, (1 << bit) - 1, -1):
                column_copy(j).wait_recv()
                column_copy(j).start()

    for bit in range(3):
        answer(bit, z >= 0)
    near_copies[1].wait_recv()
    near_copies[4].start()
    near_copies[2].wait_recv()
    near_copies[3].wait_recv()
    near_copies[5].start()

    near_copies[0].wait_recv()
    level2 = [
        terms(qc[0:128, head_cols(h)], kv2[:, head_cols(h)], kv2[:, head_cols(h + 2)], 4.0)
        for h in range(HEADS)
    ]
    near_copies[4].wait_recv()
    level3 = [
        terms(qc[128:192, head_cols(h)], kv3[:, head_cols(h)], kv3[:, head_cols(h + 2)], 8.0)
        for h in range(HEADS)
    ]
    near_copies[5].wait_recv()
    level4 = [
        terms(qc[192:224, head_cols(h)], kv4[:, head_cols(h)], kv4[:, head_cols(h + 2)], 16.0)
        for h in range(HEADS)
    ]
    for g in range(2):
        for h in range(HEADS):
            joined = tuple(x[g * 16 : (g + 1) * 16] for x in level4[h])
            joined = merge(tuple(x[g * 32 : (g + 1) * 32] for x in level3[h]), double(joined))
            joined = merge(tuple(x[g * 64 : (g + 1) * 64] for x in level2[h]), double(joined))
            joined = double(merge(level1[g, h], double(joined)))
            top, den, num = merge((state[g, h, 0], state[g, h, 1], state[g, h, 2]), joined)
            state[g, h, 0] = top
            state[g, h, 1] = den
            state[g, h, 2] = num

    def collect(bit):
        @pl.when(upper(bit))
        def _():
            for j in range((2 << bit) - 1, (1 << bit) - 1, -1):
                column_copy(j).wait_recv()

    def partial(level, queries, fields):
        return pack(
            [
                terms(
                    queries[:, head_cols(h)],
                    fields[:, head_cols(h)],
                    fields[:, head_cols(h + 2)],
                    float(2**level),
                )
                for h in range(HEADS)
            ]
        )

    answer(3, z >= 3)
    for bit in range(3):
        collect(bit)
    near_copies[6].start()
    for m in range(1, 8):
        query_copy(m).wait_recv()
    near_copies[6].wait_recv()
    for bit, first, rows in ((0, 0, 16), (1, 16, 8), (2, 24, 8)):
        queries = jnp.concatenate(
            [qg[i * SLOT + first : i * SLOT + first + rows, :] for i in range(4)], axis=0
        )
        fields = jnp.concatenate(
            [kvz[16 * bit : 16 * bit + 16, :], kvo[16 * bit : 16 * bit + 16, :]], axis=0
        )
        result = partial(5 + bit, queries, fields)
        for i in range(4):
            ret[i * SLOT + first : i * SLOT + first + rows, :] = result[i * rows : (i + 1) * rows]
    for m in (2, 4, 6):
        return_copy(m).start()
    answer(3, z < 3)
    collect(3)
    queries = []
    for m in range(8):
        queries.append(
            q8[m // 2 * 8 : m // 2 * 8 + 8, :]
            if m % 2
            else qg[m // 2 * SLOT + 24 : (m // 2 + 1) * SLOT, :]
        )
    ret8[...] = partial(8, jnp.concatenate(queries, axis=0), kvz[48:64, :])
    for m in range(1, 8):
        last_copy(m).start()
    for m in (2, 4, 6):
        return_copy(m).wait_recv()
    parts = combine([ret[0:SLOT, :]] + [got[i * SLOT : (i + 1) * SLOT, :] for i in range(1, 4)])
    spread = jnp.dot(tile[...], pack(parts), precision=HIGHEST, preferred_element_type=jnp.float32)
    for g in range(2):
        for h in range(HEADS):
            five, six, seven = (
                unpack(spread[16 * i + 8 * g : 16 * i + 8 * g + 8, :], h) for i in range(3)
            )
            joined = merge(five, merge(six, seven))
            for _ in range(5):
                joined = double(joined)
            top, den, num = merge((state[g, h, 0], state[g, h, 1], state[g, h, 2]), joined)
            state[g, h, 0] = top
            state[g, h, 1] = den
            state[g, h, 2] = num
    for m in range(1, 8):
        last_copy(m).wait_recv()
    parts = combine([ret8[0:8, :]] + [got8[m * 8 : (m + 1) * 8, :] for m in range(1, 8)])
    for g in range(2):
        attended = []
        for h in range(HEADS):
            row = tuple(x[4 + g : 5 + g, :] for x in parts[h])
            top = jnp.maximum(state[g, h, 0], row[0])
            wa = jnp.exp(state[g, h, 0] - top)
            wb = jnp.exp(row[0] - top)
            den = wa * state[g, h, 1] + wb * row[1]
            num = wa * state[g, h, 2] + wb * row[2]
            attended.append((num / den).astype(jnp.bfloat16))
        out_ref[g * GROUP : (g + 1) * GROUP, :] = jnp.dot(
            near[:GROUP, :], jnp.concatenate(attended, axis=1), preferred_element_type=jnp.float32
        ).astype(jnp.bfloat16)

    for j in range(1, 16):
        column_copy(j).wait_send()
    for copy in near_copies:
        copy.wait_send()
    for m in range(1, 8):
        query_copy(m).wait_send()
        last_copy(m).wait_send()
    for m in (2, 4, 6):
        return_copy(m).wait_send()


def on_device(queries, keys, values):
    near, far, tile = averaging()
    near = jnp.asarray(near, jnp.bfloat16)
    far = jnp.asarray(far, jnp.bfloat16)
    tile = jnp.asarray(tile, jnp.float32)
    f32, bf16 = jnp.float32, jnp.bfloat16
    whole = (TOKENS_HERE, WIDE)
    dma = pltpu.SemaphoreType.DMA
    return pl.pallas_call(
        kernel,
        out_shape=jax.ShapeDtypeStruct(whole, bf16),
        in_specs=[pl.BlockSpec(memory_space=pl.ANY)] * 6,
        out_specs=pl.BlockSpec(memory_space=pltpu.VMEM),
        scratch_shapes=[
            pltpu.VMEM(whole, bf16),
            pltpu.VMEM(whole, bf16),
            pltpu.VMEM(whole, bf16),
            pltpu.VMEM(near.shape, bf16),
            pltpu.VMEM(far.shape, bf16),
            pltpu.VMEM(tile.shape, f32),
            pltpu.VMEM((COARSE, 2 * WIDE), f32),
            pltpu.VMEM((COARSE, WIDE), f32),
            pltpu.VMEM((128, 2 * WIDE), f32),
            pltpu.VMEM((128, 2 * WIDE), f32),
            pltpu.VMEM((128, 2 * WIDE), f32),
            pltpu.VMEM((64, 2 * WIDE), f32),
            pltpu.VMEM((48, 2 * WIDE), f32),
            pltpu.VMEM((4 * SLOT, WIDE), f32),
            pltpu.VMEM((32, WIDE), f32),
            pltpu.VMEM((4 * SLOT, PACK), f32),
            pltpu.VMEM((4 * SLOT, PACK), f32),
            pltpu.VMEM((64, PACK), f32),
            pltpu.VMEM((64, PACK), f32),
            pltpu.VMEM((2, HEADS, 3, GROUP, DH), f32),
            dma((6,)),
            dma((16,)),
            dma((16,)),
            dma((7,)),
            dma((7,)),
            dma((8,)),
            dma((8,)),
            dma((8,)),
            dma((8,)),
            dma((8,)),
            dma((8,)),
        ],
        compiler_params=pltpu.CompilerParams(
            collective_id=0, has_side_effects=True, vmem_limit_bytes=54 * 2**20
        ),
    )(queries, keys, values, near, far, tile)


def solution(mesh):
    in_specs = (P("ctx", "head"), P("ctx", "head"), P("ctx", "head"))
    return jax.shard_map(
        on_device, mesh=mesh, in_specs=in_specs, out_specs=P("ctx", "head"), check_vma=False
    )
```

```python
import jax
import jax.numpy as jnp
import numpy as np
from jax import lax
from jax.experimental import pallas as pl
from jax.experimental.pallas import tpu as pltpu
from jax.sharding import PartitionSpec as P

HEADS = 2
DH = 128
GROUP = 256
TOKENS_HERE = 512
WIDE = HEADS * DH
SCALE = DH ** (-0.5)
MESH = pl.DeviceIdType.MESH
HIGHEST = lax.Precision.HIGHEST

FIRST = {2: 0, 3: 128, 4: 192, 5: 224, 6: 240, 7: 248, 8: 252}
COARSE = 256
SLOT = 32
PACK = 3 * DH


def reverse(value, bits):
    out = 0
    for _ in range(bits):
        out = out * 2 + value % 2
        value //= 2
    return out


def averaging():
    order = np.zeros((GROUP, GROUP), np.float32)
    for row in range(GROUP):
        order[row, reverse(row, 8)] = 1.0
    near = np.zeros((GROUP // 2, GROUP), np.float32)
    for row in range(GROUP // 2):
        first = reverse(row, 7) * 2
        near[row, first : first + 2] = 0.5
    far = np.zeros((COARSE, TOKENS_HERE), np.float32)
    for level in range(2, 9):
        rows = GROUP >> level
        for group in range(2):
            for row in range(rows):
                first = group * GROUP + (reverse(row, 8 - level) << level)
                far[FIRST[level] + group * rows + row, first : first + (1 << level)] = 0.5**level
    return np.concatenate([far, np.concatenate([order, np.pad(near, ((0, 128), (0, 0)))], axis=1)])


def spread_rows():
    row = lax.broadcasted_iota(jnp.int32, (48, SLOT), 0)
    col = lax.broadcasted_iota(jnp.int32, (48, SLOT), 1)
    group = row % 16 // 8
    six = 16 + group * 4 + row % 4
    seven = 24 + group * 2 + row % 2
    source = jnp.where(row < 16, row, jnp.where(row < 32, six, seven))
    return jnp.where(source == col, 1.0, 0.0)


def contract_last(a, b, precision=None):
    return lax.dot_general(
        a, b, (((1,), (1,)), ((), ())), precision=precision, preferred_element_type=jnp.float32
    )


def halves(x):
    high = x.astype(jnp.bfloat16)
    return high, (x - high.astype(jnp.float32)).astype(jnp.bfloat16)


def terms(q, k, v, weight):
    keys = k.shape[0]
    q_both = jnp.concatenate(halves(q * SCALE), axis=1)
    k_high, k_low = halves(k)
    k_high = jnp.concatenate([k_high, k_high], axis=1)
    k_low = jnp.concatenate([k_low, k_low], axis=1)
    v_both = jnp.concatenate(halves(v), axis=1)
    if keys == DH:
        scores = contract_last(q_both, jnp.concatenate([k_high, k_low], axis=0))
        scores = scores[:, :DH] + scores[:, DH:]
    else:
        scores = contract_last(q_both, k_high) + contract_last(q_both, k_low)
    top = jnp.max(scores, axis=1, keepdims=True)
    probs = jnp.exp(scores - top)
    den = weight * jnp.sum(probs, axis=1, keepdims=True)
    p_high, p_low = halves(probs * weight)
    if keys == DH:
        p_both = jnp.concatenate([p_high, p_low], axis=1)
        num = jnp.dot(
            p_both,
            jnp.concatenate([v_both, v_both], axis=0),
            preferred_element_type=jnp.float32,
        )
    else:
        num = jnp.dot(p_high, v_both, preferred_element_type=jnp.float32) + jnp.dot(
            p_low, v_both, preferred_element_type=jnp.float32
        )
    return top, den, num[:, :DH] + num[:, DH:]


def merge(a, b):
    top = jnp.maximum(a[0], b[0])
    wa = jnp.exp(a[0] - top)
    wb = jnp.exp(b[0] - top)
    return top, wa * a[1] + wb * b[1], wa * a[2] + wb * b[2]


def double(a):
    return tuple(jnp.concatenate([x, x], axis=0) for x in a)


def head_cols(h):
    return slice(h * DH, (h + 1) * DH)


def pack(parts):
    (top0, den0, num0), (top1, den1, num1) = parts
    rows = num0.shape[0]
    lane = lax.broadcasted_iota(jnp.int32, (rows, DH), 1)
    stats = jnp.where(
        lane < 64, jnp.where(lane < 32, top0, den0), jnp.where(lane < 96, top1, den1)
    )
    return jnp.concatenate([num0, num1, stats], axis=1)


def unpack(x, h):
    at = WIDE + 64 * h
    return x[:, at : at + 1], x[:, at + 32 : at + 33], x[:, head_cols(h)]


def combine(slots):
    out = []
    for h in range(HEADS):
        parts = [unpack(x, h) for x in slots]
        while len(parts) > 1:
            parts = [merge(parts[i], parts[i + 1]) for i in range(0, len(parts), 2)]
        out.append(parts[0])
    return out


def level_of(k):
    return 5 + (k.bit_length() - 1)


def kernel(
    q_hbm, k_hbm, v_hbm, mean_hbm, out_ref,
    q, k, v, mean,
    kvc, qc, kv2, kv3, kv4, kvz, kvo, qg, q8, ret, got, ret8, got8, state,
    load, z_send, z_recv, n_send, n_recv, q_send, q_recv, r_send, r_recv, e_send, e_recv,
):
    me = lax.axis_index("ctx")
    head = lax.axis_index("head")
    z = me // 8

    def peer(mask):
        return (jnp.bitwise_xor(me, mask), head)

    def side(bit):
        own = z // (1 << bit) % 2
        return (own + z // 8) % 2 if bit == 2 else own

    def upper(bit):
        return side(bit) == 1

    loads = [
        pltpu.make_async_copy(a, b, load.at[i])
        for i, (a, b) in enumerate(
            [(mean_hbm, mean), (k_hbm, k), (v_hbm, v), (q_hbm, q)]
        )
    ]
    for copy in loads:
        copy.start()

    for m in range(1, 8):
        got8[m * 8 : (m + 1) * 8, :] = jnp.zeros((8, PACK), jnp.float32)

    barrier = pltpu.get_barrier_semaphore()
    for m in range(1, 8):
        pl.semaphore_signal(barrier, inc=1, device_id=peer(m), device_id_type=MESH)
    for bit in range(3, -1, -1):

        @pl.when(jnp.logical_not(upper(bit)))
        def _(bit=bit):
            for j in range(1 << bit, 2 << bit):
                pl.semaphore_signal(barrier, inc=1, device_id=peer(8 * j), device_id_type=MESH)

    def column_copy(j):
        level = level_of(j)
        rows = TOKENS_HERE >> level
        at = (level - 5) * 16 + (j - (1 << (level - 5))) * rows
        return pltpu.make_async_remote_copy(
            kvc.at[pl.ds(FIRST[level], rows)], kvz.at[pl.ds(at, rows)],
            z_send.at[j], z_recv.at[j], device_id=peer(8 * j), device_id_type=MESH,
        )

    def near_copy(i, src, dst, mask):
        return pltpu.make_async_remote_copy(
            src, dst, n_send.at[i], n_recv.at[i], device_id=peer(mask), device_id_type=MESH
        )

    near_copies = [
        near_copy(0, kvc.at[pl.ds(FIRST[2], 128)], kv2, 1),
        near_copy(1, kvc.at[pl.ds(FIRST[3], 64)], kv3.at[pl.ds(0, 64)], 2),
        near_copy(2, kvc.at[pl.ds(FIRST[4], 32)], kv4.at[pl.ds(0, 32)], 4),
        near_copy(3, kvc.at[pl.ds(FIRST[4], 32)], kv4.at[pl.ds(32, 32)], 6),
        near_copy(4, kv3.at[pl.ds(0, 64)], kv3.at[pl.ds(64, 64)], 1),
        near_copy(5, kv4.at[pl.ds(0, 64)], kv4.at[pl.ds(64, 64)], 1),
        near_copy(6, kvz.at[pl.ds(0, 48)], kvo, 1),
    ]

    def query_copy(m):
        if m % 2 == 0:
            src, dst = qg.at[pl.ds(0, SLOT)], qg.at[pl.ds(m // 2 * SLOT, SLOT)]
        else:
            src, dst = qg.at[pl.ds(24, 8)], q8.at[pl.ds(m // 2 * 8, 8)]
        return pltpu.make_async_remote_copy(
            src, dst, q_send.at[m], q_recv.at[m], device_id=peer(m), device_id_type=MESH
        )

    def return_copy(m):
        rows = pl.ds(m // 2 * SLOT, SLOT)
        return pltpu.make_async_remote_copy(
            ret.at[rows], got.at[rows],
            r_send.at[m], r_recv.at[m], device_id=peer(m), device_id_type=MESH,
        )

    def last_copy(m):
        return pltpu.make_async_remote_copy(
            ret8.at[pl.ds(m * 8 + 4, 2)], got8.at[pl.ds(m * 8 + 4, 2)],
            e_send.at[m], e_recv.at[m], device_id=peer(m), device_id_type=MESH,
        )

    for copy in loads[:3]:
        copy.wait()
    kvc[:, :WIDE] = jnp.dot(mean[:COARSE, :], k[...], preferred_element_type=jnp.float32)
    kvc[:, WIDE:] = jnp.dot(mean[:COARSE, :], v[...], preferred_element_type=jnp.float32)

    pl.semaphore_wait(barrier, 7 + sum(side(bit) << bit for bit in range(4)))
    for bit in range(3, -1, -1):

        @pl.when(upper(bit))
        def _(bit=bit):
            for j in range(1 << bit, 2 << bit):
                column_copy(j).start()

    for copy in near_copies[:4]:
        copy.start()
    loads[3].wait()
    qc[...] = jnp.dot(mean[:COARSE, :], q[...], preferred_element_type=jnp.float32)
    qg[0:SLOT, :] = qc[FIRST[5] : COARSE, :]
    for m in range(1, 8):
        query_copy(m).start()

    ones = jnp.ones((GROUP, DH), jnp.bfloat16)
    q_near, k_near, v_near = [], [], []
    for g in range(2):
        rows = slice(g * GROUP, (g + 1) * GROUP)
        pair = mean[COARSE : COARSE + 128, GROUP:]
        q_near.append(jnp.dot(pair, q[rows, :], preferred_element_type=jnp.float32))
        k_near.append(jnp.dot(pair, k[rows, :], preferred_element_type=jnp.float32))
        v_near.append(jnp.dot(pair, v[rows, :], preferred_element_type=jnp.float32))
    level1 = {}
    for g in range(2):
        rows = slice(g * GROUP, (g + 1) * GROUP)
        ordered = jnp.dot(
            mean[COARSE:, :GROUP], q[rows, :], preferred_element_type=jnp.float32
        ).astype(jnp.bfloat16)
        for h in range(HEADS):
            cols = head_cols(h)
            scores = contract_last(ordered[:, cols], k[rows, cols]) * SCALE
            top = jnp.max(scores, axis=1, keepdims=True)
            probs = jnp.exp(scores - top)
            high = probs.astype(jnp.bfloat16)
            low = (probs - high.astype(jnp.float32)).astype(jnp.bfloat16)
            wide = jnp.concatenate([v[rows, cols], ones], axis=1)
            both = jnp.dot(high, wide, preferred_element_type=jnp.float32) + jnp.dot(
                low, wide, preferred_element_type=jnp.float32
            )
            state[g, h, 0] = jnp.broadcast_to(top, (GROUP, DH))
            state[g, h, 1] = both[:, DH:]
            state[g, h, 2] = both[:, :DH]
            level1[g, h] = terms(
                q_near[g][:, cols], k_near[1 - g][:, cols], v_near[1 - g][:, cols], 2.0
            )

    def answer(bit, here):
        @pl.when(jnp.logical_and(here, jnp.logical_not(upper(bit))))
        def _():
            for j in range((2 << bit) - 1, (1 << bit) - 1, -1):
                column_copy(j).wait_recv()
                column_copy(j).start()

    for bit in range(2):
        answer(bit, z >= 0)
    answer(2, z >= 3)
    near_copies[1].wait_recv()
    near_copies[4].start()
    near_copies[2].wait_recv()
    near_copies[3].wait_recv()
    near_copies[5].start()

    near_copies[0].wait_recv()
    level2 = [
        terms(qc[0:128, head_cols(h)], kv2[:, head_cols(h)], kv2[:, head_cols(h + 2)], 4.0)
        for h in range(HEADS)
    ]
    near_copies[4].wait_recv()
    level3 = [
        terms(qc[128:192, head_cols(h)], kv3[:, head_cols(h)], kv3[:, head_cols(h + 2)], 8.0)
        for h in range(HEADS)
    ]
    near_copies[5].wait_recv()
    level4 = [
        terms(qc[192:224, head_cols(h)], kv4[:, head_cols(h)], kv4[:, head_cols(h + 2)], 16.0)
        for h in range(HEADS)
    ]
    answer(2, z < 3)
    for g in range(2):
        for h in range(HEADS):
            joined = tuple(x[g * 16 : (g + 1) * 16] for x in level4[h])
            joined = merge(tuple(x[g * 32 : (g + 1) * 32] for x in level3[h]), double(joined))
            joined = merge(tuple(x[g * 64 : (g + 1) * 64] for x in level2[h]), double(joined))
            joined = double(merge(level1[g, h], double(joined)))
            top, den, num = merge((state[g, h, 0], state[g, h, 1], state[g, h, 2]), joined)
            state[g, h, 0] = top
            state[g, h, 1] = den
            state[g, h, 2] = num

    def collect(bit):
        @pl.when(upper(bit))
        def _():
            for j in range((2 << bit) - 1, (1 << bit) - 1, -1):
                column_copy(j).wait_recv()

    def partial(level, queries, fields):
        return pack(
            [
                terms(
                    queries[:, head_cols(h)],
                    fields[:, head_cols(h)],
                    fields[:, head_cols(h + 2)],
                    float(2**level),
                )
                for h in range(HEADS)
            ]
        )

    answer(3, z >= 3)
    for bit in range(3):
        collect(bit)
    near_copies[6].start()
    for m in range(1, 8):
        query_copy(m).wait_recv()
    near_copies[6].wait_recv()
    for bit, first, rows in ((0, 0, 16), (1, 16, 8), (2, 24, 8)):
        queries = jnp.concatenate(
            [qg[i * SLOT + first : i * SLOT + first + rows, :] for i in range(4)], axis=0
        )
        fields = jnp.concatenate(
            [kvz[16 * bit : 16 * bit + 16, :], kvo[16 * bit : 16 * bit + 16, :]], axis=0
        )
        result = partial(5 + bit, queries, fields)
        for i in range(4):
            ret[i * SLOT + first : i * SLOT + first + rows, :] = result[i * rows : (i + 1) * rows]
    for m in (2, 4, 6):
        return_copy(m).start()
    answer(3, z < 3)
    collect(3)
    queries = []
    for m in range(8):
        queries.append(
            q8[m // 2 * 8 : m // 2 * 8 + 8, :]
            if m % 2
            else qg[m // 2 * SLOT + 24 : (m // 2 + 1) * SLOT, :]
        )
    ret8[...] = partial(8, jnp.concatenate(queries, axis=0), kvz[48:64, :])
    for m in range(1, 8):
        last_copy(m).start()
    for m in (2, 4, 6):
        return_copy(m).wait_recv()
    parts = combine([ret[0:SLOT, :]] + [got[i * SLOT : (i + 1) * SLOT, :] for i in range(1, 4)])
    spread = jnp.dot(spread_rows(), pack(parts), precision=HIGHEST, preferred_element_type=jnp.float32)
    for g in range(2):
        for h in range(HEADS):
            five, six, seven = (
                unpack(spread[16 * i + 8 * g : 16 * i + 8 * g + 8, :], h) for i in range(3)
            )
            joined = merge(five, merge(six, seven))
            for _ in range(5):
                joined = double(joined)
            top, den, num = merge((state[g, h, 0], state[g, h, 1], state[g, h, 2]), joined)
            state[g, h, 0] = top
            state[g, h, 1] = den
            state[g, h, 2] = num
    for m in range(1, 8):
        last_copy(m).wait_recv()
    parts = combine([ret8[0:8, :]] + [got8[m * 8 : (m + 1) * 8, :] for m in range(1, 8)])
    for g in range(2):
        attended = []
        for h in range(HEADS):
            row = tuple(x[4 + g : 5 + g, :] for x in parts[h])
            top = jnp.maximum(state[g, h, 0], row[0])
            wa = jnp.exp(state[g, h, 0] - top)
            wb = jnp.exp(row[0] - top)
            den = wa * state[g, h, 1] + wb * row[1]
            num = wa * state[g, h, 2] + wb * row[2]
            attended.append((num / den).astype(jnp.bfloat16))
        out_ref[g * GROUP : (g + 1) * GROUP, :] = jnp.dot(
            mean[COARSE:, :GROUP], jnp.concatenate(attended, axis=1), preferred_element_type=jnp.float32
        ).astype(jnp.bfloat16)

    for j in range(1, 16):
        column_copy(j).wait_send()
    for copy in near_copies:
        copy.wait_send()
    for m in range(1, 8):
        query_copy(m).wait_send()
        last_copy(m).wait_send()
    for m in (2, 4, 6):
        return_copy(m).wait_send()


def on_device(queries, keys, values):
    mean = jnp.asarray(averaging(), jnp.bfloat16)
    f32, bf16 = jnp.float32, jnp.bfloat16
    whole = (TOKENS_HERE, WIDE)
    dma = pltpu.SemaphoreType.DMA
    return pl.pallas_call(
        kernel,
        out_shape=jax.ShapeDtypeStruct(whole, bf16),
        in_specs=[pl.BlockSpec(memory_space=pl.ANY)] * 4,
        out_specs=pl.BlockSpec(memory_space=pltpu.VMEM),
        scratch_shapes=[
            pltpu.VMEM(whole, bf16),
            pltpu.VMEM(whole, bf16),
            pltpu.VMEM(whole, bf16),
            pltpu.VMEM(mean.shape, bf16),
            pltpu.VMEM((COARSE, 2 * WIDE), f32),
            pltpu.VMEM((COARSE, WIDE), f32),
            pltpu.VMEM((128, 2 * WIDE), f32),
            pltpu.VMEM((128, 2 * WIDE), f32),
            pltpu.VMEM((128, 2 * WIDE), f32),
            pltpu.VMEM((64, 2 * WIDE), f32),
            pltpu.VMEM((48, 2 * WIDE), f32),
            pltpu.VMEM((4 * SLOT, WIDE), f32),
            pltpu.VMEM((32, WIDE), f32),
            pltpu.VMEM((4 * SLOT, PACK), f32),
            pltpu.VMEM((4 * SLOT, PACK), f32),
            pltpu.VMEM((64, PACK), f32),
            pltpu.VMEM((64, PACK), f32),
            pltpu.VMEM((2, HEADS, 3, GROUP, DH), f32),
            dma((4,)),
            dma((16,)),
            dma((16,)),
            dma((7,)),
            dma((7,)),
            dma((8,)),
            dma((8,)),
            dma((8,)),
            dma((8,)),
            dma((8,)),
            dma((8,)),
        ],
        compiler_params=pltpu.CompilerParams(
            collective_id=0, has_side_effects=True, vmem_limit_bytes=54900 * 1024
        ),
    )(queries, keys, values, mean)


def solution(mesh):
    in_specs = (P("ctx", "head"), P("ctx", "head"), P("ctx", "head"))
    return jax.shard_map(
        on_device, mesh=mesh, in_specs=in_specs, out_specs=P("ctx", "head"), check_vma=False
    )
```

```python
import jax
import jax.numpy as jnp
import numpy as np
from jax import lax
from jax.experimental import pallas as pl
from jax.experimental.pallas import tpu as pltpu
from jax.sharding import PartitionSpec as P

HEADS = 2
DH = 128
GROUP = 256
TOKENS_HERE = 512
WIDE = HEADS * DH
SCALE = DH ** (-0.5)
MESH = pl.DeviceIdType.MESH
HIGHEST = lax.Precision.HIGHEST

FIRST = {2: 0, 3: 128, 4: 192, 5: 224, 6: 240, 7: 248, 8: 252}
COARSE = 256
SLOT = 32
PACK = 3 * DH


def reverse(value, bits):
    out = 0
    for _ in range(bits):
        out = out * 2 + value % 2
        value //= 2
    return out


def averaging():
    order = np.zeros((GROUP, GROUP), np.float32)
    for row in range(GROUP):
        order[row, reverse(row, 8)] = 1.0
    near = np.zeros((GROUP // 2, GROUP), np.float32)
    for row in range(GROUP // 2):
        first = reverse(row, 7) * 2
        near[row, first : first + 2] = 0.5
    far = np.zeros((COARSE, TOKENS_HERE), np.float32)
    for level in range(2, 9):
        rows = GROUP >> level
        for group in range(2):
            for row in range(rows):
                first = group * GROUP + (reverse(row, 8 - level) << level)
                far[FIRST[level] + group * rows + row, first : first + (1 << level)] = 0.5**level
    return np.concatenate([far, np.concatenate([order, np.pad(near, ((0, 128), (0, 0)))], axis=1)])


def spread_rows():
    row = lax.broadcasted_iota(jnp.int32, (48, SLOT), 0)
    col = lax.broadcasted_iota(jnp.int32, (48, SLOT), 1)
    group = row % 16 // 8
    six = 16 + group * 4 + row % 4
    seven = 24 + group * 2 + row % 2
    source = jnp.where(row < 16, row, jnp.where(row < 32, six, seven))
    return jnp.where(source == col, 1.0, 0.0)


def contract_last(a, b, precision=None):
    return lax.dot_general(
        a, b, (((1,), (1,)), ((), ())), precision=precision, preferred_element_type=jnp.float32
    )


def halves(x):
    high = x.astype(jnp.bfloat16)
    return high, (x - high.astype(jnp.float32)).astype(jnp.bfloat16)


def terms(q, k, v, weight):
    keys = k.shape[0]
    q_both = jnp.concatenate(halves(q * SCALE), axis=1)
    k_high, k_low = halves(k)
    k_high = jnp.concatenate([k_high, k_high], axis=1)
    k_low = jnp.concatenate([k_low, k_low], axis=1)
    v_both = jnp.concatenate(halves(v), axis=1)
    if keys == DH:
        scores = contract_last(q_both, jnp.concatenate([k_high, k_low], axis=0))
        scores = scores[:, :DH] + scores[:, DH:]
    else:
        scores = contract_last(q_both, k_high) + contract_last(q_both, k_low)
    top = jnp.max(scores, axis=1, keepdims=True)
    probs = jnp.exp(scores - top)
    den = weight * jnp.sum(probs, axis=1, keepdims=True)
    p_high, p_low = halves(probs * weight)
    if keys == DH:
        p_both = jnp.concatenate([p_high, p_low], axis=1)
        num = jnp.dot(
            p_both,
            jnp.concatenate([v_both, v_both], axis=0),
            preferred_element_type=jnp.float32,
        )
    else:
        num = jnp.dot(p_high, v_both, preferred_element_type=jnp.float32) + jnp.dot(
            p_low, v_both, preferred_element_type=jnp.float32
        )
    return top, den, num[:, :DH] + num[:, DH:]


def merge(a, b):
    top = jnp.maximum(a[0], b[0])
    wa = jnp.exp(a[0] - top)
    wb = jnp.exp(b[0] - top)
    return top, wa * a[1] + wb * b[1], wa * a[2] + wb * b[2]


def double(a):
    return tuple(jnp.concatenate([x, x], axis=0) for x in a)


def head_cols(h):
    return slice(h * DH, (h + 1) * DH)


def pack(parts):
    (top0, den0, num0), (top1, den1, num1) = parts
    rows = num0.shape[0]
    lane = lax.broadcasted_iota(jnp.int32, (rows, DH), 1)
    stats = jnp.where(
        lane < 64, jnp.where(lane < 32, top0, den0), jnp.where(lane < 96, top1, den1)
    )
    return jnp.concatenate([num0, num1, stats], axis=1)


def unpack(x, h):
    at = WIDE + 64 * h
    return x[:, at : at + 1], x[:, at + 32 : at + 33], x[:, head_cols(h)]


def total(items):
    while len(items) > 1:
        items = [items[i] + items[i + 1] for i in range(0, len(items), 2)]
    return items[0]


def combine(slots):
    out = []
    for h in range(HEADS):
        parts = [unpack(x, h) for x in slots]
        tops = [p[0] for p in parts]
        while len(tops) > 1:
            tops = [jnp.maximum(tops[i], tops[i + 1]) for i in range(0, len(tops), 2)]
        scaled = [jnp.exp(p[0] - tops[0]) for p in parts]
        out.append(
            (
                tops[0],
                total([w * p[1] for w, p in zip(scaled, parts)]),
                total([w * p[2] for w, p in zip(scaled, parts)]),
            )
        )
    return out


def level_of(k):
    return 5 + (k.bit_length() - 1)


def kernel(
    q_hbm, k_hbm, v_hbm, mean_hbm, out_ref,
    q, k, v, mean,
    kvc, qc, kv2, kv3, kv4, kvz, kvo, qg, q8, ret, got, ret8, got8, state,
    load, z_send, z_recv, n_send, n_recv, q_send, q_recv, r_send, r_recv, e_send, e_recv,
):
    me = lax.axis_index("ctx")
    head = lax.axis_index("head")
    z = me // 8

    def peer(mask):
        return (jnp.bitwise_xor(me, mask), head)

    def upper(bit):
        return z // (1 << bit) % 2 == 1

    loads = [
        pltpu.make_async_copy(a, b, load.at[i])
        for i, (a, b) in enumerate(
            [
                (mean_hbm.at[pl.ds(0, COARSE)], mean.at[pl.ds(0, COARSE)]),
                (k_hbm, k),
                (v_hbm, v),
                (q_hbm, q),
                (mean_hbm.at[pl.ds(COARSE, COARSE)], mean.at[pl.ds(COARSE, COARSE)]),
            ]
        )
    ]
    for copy in loads[:3]:
        copy.start()

    for m in range(1, 8):
        got8[m * 8 : (m + 1) * 8, :] = jnp.zeros((8, PACK), jnp.float32)

    barrier = pltpu.get_barrier_semaphore()
    for m in range(1, 8):
        pl.semaphore_signal(barrier, inc=1, device_id=peer(m), device_id_type=MESH)
    for bit in range(3, -1, -1):

        @pl.when(jnp.logical_not(upper(bit)))
        def _(bit=bit):
            for j in range(1 << bit, 2 << bit):
                pl.semaphore_signal(barrier, inc=1, device_id=peer(8 * j), device_id_type=MESH)

    def column_copy(j):
        level = level_of(j)
        rows = TOKENS_HERE >> level
        at = (level - 5) * 16 + (j - (1 << (level - 5))) * rows
        return pltpu.make_async_remote_copy(
            kvc.at[pl.ds(FIRST[level], rows)], kvz.at[pl.ds(at, rows)],
            z_send.at[j], z_recv.at[j], device_id=peer(8 * j), device_id_type=MESH,
        )

    def near_copy(i, src, dst, mask):
        return pltpu.make_async_remote_copy(
            src, dst, n_send.at[i], n_recv.at[i], device_id=peer(mask), device_id_type=MESH
        )

    near_copies = [
        near_copy(0, kvc.at[pl.ds(FIRST[2], 128)], kv2, 1),
        near_copy(1, kvc.at[pl.ds(FIRST[3], 64)], kv3.at[pl.ds(0, 64)], 2),
        near_copy(2, kvc.at[pl.ds(FIRST[4], 32)], kv4.at[pl.ds(0, 32)], 4),
        near_copy(3, kvc.at[pl.ds(FIRST[4], 32)], kv4.at[pl.ds(32, 32)], 6),
        near_copy(4, kv3.at[pl.ds(0, 64)], kv3.at[pl.ds(64, 64)], 1),
        near_copy(5, kv4.at[pl.ds(0, 64)], kv4.at[pl.ds(64, 64)], 1),
        near_copy(6, kvz.at[pl.ds(0, 32)], kvo.at[pl.ds(0, 32)], 1),
        near_copy(7, kvz.at[pl.ds(32, 16)], kvo.at[pl.ds(32, 16)], 1),
    ]

    def query_copy(m):
        if m % 2 == 0:
            src, dst = qg.at[pl.ds(0, SLOT)], qg.at[pl.ds(m // 2 * SLOT, SLOT)]
        else:
            src, dst = qg.at[pl.ds(24, 8)], q8.at[pl.ds(m // 2 * 8, 8)]
        return pltpu.make_async_remote_copy(
            src, dst, q_send.at[m], q_recv.at[m], device_id=peer(m), device_id_type=MESH
        )

    def return_copy(m):
        rows = pl.ds(m // 2 * SLOT + 24 * (m % 2), 8 if m % 2 else 24)
        return pltpu.make_async_remote_copy(
            ret.at[rows], got.at[rows],
            r_send.at[m], r_recv.at[m], device_id=peer(m - m % 2), device_id_type=MESH,
        )

    def last_copy(m):
        return pltpu.make_async_remote_copy(
            ret8.at[pl.ds(m * 8 + 4, 2)], got8.at[pl.ds(m * 8 + 4, 2)],
            e_send.at[m], e_recv.at[m], device_id=peer(m), device_id_type=MESH,
        )

    for copy in loads[:3]:
        copy.wait()
    for copy in loads[3:]:
        copy.start()
    kvc[:, :WIDE] = jnp.dot(mean[:COARSE, :], k[...], preferred_element_type=jnp.float32)
    kvc[:, WIDE:] = jnp.dot(mean[:COARSE, :], v[...], preferred_element_type=jnp.float32)

    pl.semaphore_wait(barrier, 7 + z)
    for bit in range(3, -1, -1):

        @pl.when(upper(bit))
        def _(bit=bit):
            for j in range(1 << bit, 2 << bit):
                column_copy(j).start()

    for copy in near_copies[:4]:
        copy.start()
    loads[3].wait()
    loads[4].wait()
    qc[...] = jnp.dot(mean[:COARSE, :], q[...], preferred_element_type=jnp.float32)
    qg[0:SLOT, :] = qc[FIRST[5] : COARSE, :]
    for m in range(1, 8):
        query_copy(m).start()

    ones = jnp.ones((GROUP, DH), jnp.bfloat16)
    q_near, k_near, v_near = [], [], []
    for g in range(2):
        rows = slice(g * GROUP, (g + 1) * GROUP)
        pair = mean[COARSE : COARSE + 128, GROUP:]
        q_near.append(jnp.dot(pair, q[rows, :], preferred_element_type=jnp.float32))
        k_near.append(jnp.dot(pair, k[rows, :], preferred_element_type=jnp.float32))
        v_near.append(jnp.dot(pair, v[rows, :], preferred_element_type=jnp.float32))
    level1 = {}
    for g in range(2):
        rows = slice(g * GROUP, (g + 1) * GROUP)
        ordered = jnp.dot(
            mean[COARSE:, :GROUP], q[rows, :], preferred_element_type=jnp.float32
        ).astype(jnp.bfloat16)
        for h in range(HEADS):
            cols = head_cols(h)
            scores = contract_last(ordered[:, cols], k[rows, cols]) * SCALE
            top = jnp.max(scores, axis=1, keepdims=True)
            probs = jnp.exp(scores - top)
            high = probs.astype(jnp.bfloat16)
            low = (probs - high.astype(jnp.float32)).astype(jnp.bfloat16)
            wide = jnp.concatenate([v[rows, cols], ones], axis=1)
            both = jnp.dot(high, wide, preferred_element_type=jnp.float32) + jnp.dot(
                low, wide, preferred_element_type=jnp.float32
            )
            state[g, h, 0] = jnp.broadcast_to(top, (GROUP, DH))
            state[g, h, 1] = both[:, DH:]
            state[g, h, 2] = both[:, :DH]
            level1[g, h] = terms(
                q_near[g][:, cols], k_near[1 - g][:, cols], v_near[1 - g][:, cols], 2.0
            )

    def answer(bit, here):
        @pl.when(jnp.logical_and(here, jnp.logical_not(upper(bit))))
        def _():
            for j in range((2 << bit) - 1, (1 << bit) - 1, -1):
                column_copy(j).wait_recv()
                column_copy(j).start()

    for bit in range(2):
        answer(bit, z >= 0)
    answer(2, z >= 3)
    near_copies[1].wait_recv()
    near_copies[4].start()
    near_copies[2].wait_recv()
    near_copies[3].wait_recv()
    near_copies[5].start()

    near_copies[0].wait_recv()
    level2 = [
        terms(qc[0:128, head_cols(h)], kv2[:, head_cols(h)], kv2[:, head_cols(h + 2)], 4.0)
        for h in range(HEADS)
    ]
    near_copies[4].wait_recv()
    level3 = [
        terms(qc[128:192, head_cols(h)], kv3[:, head_cols(h)], kv3[:, head_cols(h + 2)], 8.0)
        for h in range(HEADS)
    ]
    near_copies[5].wait_recv()
    level4 = [
        terms(qc[192:224, head_cols(h)], kv4[:, head_cols(h)], kv4[:, head_cols(h + 2)], 16.0)
        for h in range(HEADS)
    ]
    answer(2, z < 3)
    for g in range(2):
        for h in range(HEADS):
            joined = tuple(x[g * 16 : (g + 1) * 16] for x in level4[h])
            joined = merge(tuple(x[g * 32 : (g + 1) * 32] for x in level3[h]), double(joined))
            joined = merge(tuple(x[g * 64 : (g + 1) * 64] for x in level2[h]), double(joined))
            joined = double(merge(level1[g, h], double(joined)))
            top, den, num = merge((state[g, h, 0], state[g, h, 1], state[g, h, 2]), joined)
            state[g, h, 0] = top
            state[g, h, 1] = den
            state[g, h, 2] = num

    def collect(bit):
        @pl.when(upper(bit))
        def _():
            for j in range((2 << bit) - 1, (1 << bit) - 1, -1):
                column_copy(j).wait_recv()

    def partial(level, queries, fields):
        return pack(
            [
                terms(
                    queries[:, head_cols(h)],
                    fields[:, head_cols(h)],
                    fields[:, head_cols(h + 2)],
                    float(2**level),
                )
                for h in range(HEADS)
            ]
        )

    answer(3, z >= 4)
    collect(0)
    collect(1)
    near_copies[6].start()
    for m in range(1, 8):
        query_copy(m).wait_recv()

    def return_level(bit):
        first, rows = ((0, 16), (16, 8), (24, 8))[bit]
        queries = jnp.concatenate(
            [qg[i * SLOT + first : i * SLOT + first + rows, :] for i in range(4)], axis=0
        )
        fields = jnp.concatenate(
            [kvz[16 * bit : 16 * bit + 16, :], kvo[16 * bit : 16 * bit + 16, :]], axis=0
        )
        result = partial(5 + bit, queries, fields)
        for i in range(4):
            ret[i * SLOT + first : i * SLOT + first + rows, :] = result[i * rows : (i + 1) * rows]

    near_copies[6].wait_recv()
    return_level(0)
    return_level(1)
    for m in (4, 2, 6):
        return_copy(m).start()
    collect(2)
    near_copies[7].start()
    near_copies[7].wait_recv()
    return_level(2)
    for m in (5, 3, 7):
        return_copy(m).start()
    answer(3, z < 4)
    collect(3)
    queries = []
    for m in range(8):
        queries.append(
            q8[m // 2 * 8 : m // 2 * 8 + 8, :]
            if m % 2
            else qg[m // 2 * SLOT + 24 : (m // 2 + 1) * SLOT, :]
        )
    ret8[...] = partial(8, jnp.concatenate(queries, axis=0), kvz[48:64, :])
    for m in (4, 5, 2, 3, 6, 7, 1):
        last_copy(m).start()
    for m in range(2, 8):
        return_copy(m).wait_recv()
    parts = combine([ret[0:SLOT, :]] + [got[i * SLOT : (i + 1) * SLOT, :] for i in range(1, 4)])
    spread = jnp.dot(spread_rows(), pack(parts), precision=HIGHEST, preferred_element_type=jnp.float32)
    for g in range(2):
        for h in range(HEADS):
            five, six, seven = (
                unpack(spread[16 * i + 8 * g : 16 * i + 8 * g + 8, :], h) for i in range(3)
            )
            joined = merge(five, merge(six, seven))
            for _ in range(5):
                joined = double(joined)
            top, den, num = merge((state[g, h, 0], state[g, h, 1], state[g, h, 2]), joined)
            state[g, h, 0] = top
            state[g, h, 1] = den
            state[g, h, 2] = num
    for j in range(1, 16):
        column_copy(j).wait_send()
    for copy in near_copies:
        copy.wait_send()
    for m in range(1, 8):
        query_copy(m).wait_send()
    for m in range(2, 8):
        return_copy(m).wait_send()
    for m in range(1, 8):
        last_copy(m).wait()
    parts = combine([ret8[0:8, :]] + [got8[m * 8 : (m + 1) * 8, :] for m in range(1, 8)])
    for g in range(2):
        attended = []
        for h in range(HEADS):
            row = tuple(x[4 + g : 5 + g, :] for x in parts[h])
            gap = row[0] - state[g, h, 0]
            small = jnp.exp(-jnp.abs(gap))
            wa = jnp.where(gap > 0.0, small, 1.0)
            wb = jnp.where(gap > 0.0, 1.0, small)
            inverse = 1.0 / (wa * state[g, h, 1] + wb * row[1])
            joined = (wa * inverse) * state[g, h, 2] + (wb * inverse) * row[2]
            attended.append(joined.astype(jnp.bfloat16))
        out_ref[g * GROUP : (g + 1) * GROUP, :] = jnp.dot(
            mean[COARSE:, :GROUP], jnp.concatenate(attended, axis=1), preferred_element_type=jnp.float32
        ).astype(jnp.bfloat16)


def on_device(queries, keys, values):
    mean = jnp.asarray(averaging(), jnp.bfloat16)
    f32, bf16 = jnp.float32, jnp.bfloat16
    whole = (TOKENS_HERE, WIDE)
    dma = pltpu.SemaphoreType.DMA
    return pl.pallas_call(
        kernel,
        out_shape=jax.ShapeDtypeStruct(whole, bf16),
        in_specs=[pl.BlockSpec(memory_space=pl.ANY)] * 4,
        out_specs=pl.BlockSpec(memory_space=pltpu.VMEM),
        scratch_shapes=[
            pltpu.VMEM(whole, bf16),
            pltpu.VMEM(whole, bf16),
            pltpu.VMEM(whole, bf16),
            pltpu.VMEM(mean.shape, bf16),
            pltpu.VMEM((COARSE, 2 * WIDE), f32),
            pltpu.VMEM((COARSE, WIDE), f32),
            pltpu.VMEM((128, 2 * WIDE), f32),
            pltpu.VMEM((128, 2 * WIDE), f32),
            pltpu.VMEM((128, 2 * WIDE), f32),
            pltpu.VMEM((64, 2 * WIDE), f32),
            pltpu.VMEM((48, 2 * WIDE), f32),
            pltpu.VMEM((4 * SLOT, WIDE), f32),
            pltpu.VMEM((32, WIDE), f32),
            pltpu.VMEM((4 * SLOT, PACK), f32),
            pltpu.VMEM((4 * SLOT, PACK), f32),
            pltpu.VMEM((64, PACK), f32),
            pltpu.VMEM((64, PACK), f32),
            pltpu.VMEM((2, HEADS, 3, GROUP, DH), f32),
            dma((5,)),
            dma((16,)),
            dma((16,)),
            dma((8,)),
            dma((8,)),
            dma((8,)),
            dma((8,)),
            dma((8,)),
            dma((8,)),
            dma((8,)),
            dma((8,)),
        ],
        compiler_params=pltpu.CompilerParams(
            collective_id=0, has_side_effects=True, vmem_limit_bytes=54900 * 1024
        ),
    )(queries, keys, values, mean)


def solution(mesh):
    in_specs = (P("ctx", "head"), P("ctx", "head"), P("ctx", "head"))
    return jax.shard_map(
        on_device, mesh=mesh, in_specs=in_specs, out_specs=P("ctx", "head"), check_vma=False
    )
```

```python
import jax
import jax.numpy as jnp
import numpy as np
from jax import lax
from jax.experimental import pallas as pl
from jax.experimental.pallas import tpu as pltpu
from jax.sharding import PartitionSpec as P

HEADS = 2
DH = 128
GROUP = 256
TOKENS_HERE = 512
WIDE = HEADS * DH
SCALE = DH ** (-0.5)
MESH = pl.DeviceIdType.MESH
HIGHEST = lax.Precision.HIGHEST

FIRST = {2: 0, 3: 128, 4: 192, 5: 224, 6: 240, 7: 248, 8: 252}
COARSE = 256
SLOT = 32
PACK = 3 * DH


def reverse(value, bits):
    out = 0
    for _ in range(bits):
        out = out * 2 + value % 2
        value //= 2
    return out


def averaging():
    order = np.zeros((GROUP, GROUP), np.float32)
    for row in range(GROUP):
        order[row, reverse(row, 8)] = 1.0
    near = np.zeros((GROUP // 2, GROUP), np.float32)
    for row in range(GROUP // 2):
        first = reverse(row, 7) * 2
        near[row, first : first + 2] = 0.5
    far = np.zeros((COARSE, TOKENS_HERE), np.float32)
    for level in range(2, 9):
        rows = GROUP >> level
        for group in range(2):
            for row in range(rows):
                first = group * GROUP + (reverse(row, 8 - level) << level)
                far[FIRST[level] + group * rows + row, first : first + (1 << level)] = 0.5**level
    return np.concatenate([far, np.concatenate([order, np.pad(near, ((0, 128), (0, 0)))], axis=1)])


def spread_rows():
    row = lax.broadcasted_iota(jnp.int32, (48, SLOT), 0)
    col = lax.broadcasted_iota(jnp.int32, (48, SLOT), 1)
    group = row % 16 // 8
    six = 16 + group * 4 + row % 4
    seven = 24 + group * 2 + row % 2
    source = jnp.where(row < 16, row, jnp.where(row < 32, six, seven))
    return jnp.where(source == col, 1.0, 0.0)


def contract_last(a, b, precision=None):
    return lax.dot_general(
        a, b, (((1,), (1,)), ((), ())), precision=precision, preferred_element_type=jnp.float32
    )


def halves(x):
    high = x.astype(jnp.bfloat16)
    return high, (x - high.astype(jnp.float32)).astype(jnp.bfloat16)


def terms(q, k, v, weight):
    keys = k.shape[0]
    q_both = jnp.concatenate(halves(q * SCALE), axis=1)
    k_high, k_low = halves(k)
    k_high = jnp.concatenate([k_high, k_high], axis=1)
    k_low = jnp.concatenate([k_low, k_low], axis=1)
    v_both = jnp.concatenate(halves(v), axis=1)
    if keys == DH:
        scores = contract_last(q_both, jnp.concatenate([k_high, k_low], axis=0))
        scores = scores[:, :DH] + scores[:, DH:]
    else:
        scores = contract_last(q_both, k_high) + contract_last(q_both, k_low)
    top = jnp.max(scores, axis=1, keepdims=True)
    probs = jnp.exp(scores - top)
    den = weight * jnp.sum(probs, axis=1, keepdims=True)
    p_high, p_low = halves(probs * weight)
    if keys == DH:
        p_both = jnp.concatenate([p_high, p_low], axis=1)
        num = jnp.dot(
            p_both,
            jnp.concatenate([v_both, v_both], axis=0),
            preferred_element_type=jnp.float32,
        )
    else:
        num = jnp.dot(p_high, v_both, preferred_element_type=jnp.float32) + jnp.dot(
            p_low, v_both, preferred_element_type=jnp.float32
        )
    return top, den, num[:, :DH] + num[:, DH:]


def merge(a, b):
    top = jnp.maximum(a[0], b[0])
    wa = jnp.exp(a[0] - top)
    wb = jnp.exp(b[0] - top)
    return top, wa * a[1] + wb * b[1], wa * a[2] + wb * b[2]


def double(a):
    return tuple(jnp.concatenate([x, x], axis=0) for x in a)


def head_cols(h):
    return slice(h * DH, (h + 1) * DH)


def pack(parts):
    (top0, den0, num0), (top1, den1, num1) = parts
    rows = num0.shape[0]
    lane = lax.broadcasted_iota(jnp.int32, (rows, DH), 1)
    stats = jnp.where(
        lane < 64, jnp.where(lane < 32, top0, den0), jnp.where(lane < 96, top1, den1)
    )
    return jnp.concatenate([num0, num1, stats], axis=1)


def unpack(x, h):
    at = WIDE + 64 * h
    return x[:, at : at + 1], x[:, at + 32 : at + 33], x[:, head_cols(h)]


def total(items):
    while len(items) > 1:
        items = [items[i] + items[i + 1] for i in range(0, len(items), 2)]
    return items[0]


def combine(slots):
    out = []
    for h in range(HEADS):
        parts = [unpack(x, h) for x in slots]
        tops = [p[0] for p in parts]
        while len(tops) > 1:
            tops = [jnp.maximum(tops[i], tops[i + 1]) for i in range(0, len(tops), 2)]
        scaled = [jnp.exp(p[0] - tops[0]) for p in parts]
        out.append(
            (
                tops[0],
                total([w * p[1] for w, p in zip(scaled, parts)]),
                total([w * p[2] for w, p in zip(scaled, parts)]),
            )
        )
    return out


def level_of(k):
    return 5 + (k.bit_length() - 1)


def kernel(
    q_hbm, k_hbm, v_hbm, mean_hbm, out_ref,
    q, k, v, mean,
    kvc, qc, kv2, kv3, kv4, kvz, kvo, qg, q8, ret, got, ret8, got8, state,
    load, z_send, z_recv, n_send, n_recv, q_send, q_recv, r_send, r_recv, e_send, e_recv,
):
    me = lax.axis_index("ctx")
    head = lax.axis_index("head")
    z = me // 8

    def peer(mask):
        return (jnp.bitwise_xor(me, mask), head)

    def upper(bit):
        return z // (1 << bit) % 2 == 1

    loads = [
        pltpu.make_async_copy(a, b, load.at[i])
        for i, (a, b) in enumerate(
            [
                (mean_hbm.at[pl.ds(FIRST[5], SLOT)], mean.at[pl.ds(FIRST[5], SLOT)]),
                (k_hbm, k),
                (v_hbm, v),
                (q_hbm, q),
                (mean_hbm.at[pl.ds(COARSE, COARSE)], mean.at[pl.ds(COARSE, COARSE)]),
                (mean_hbm.at[pl.ds(0, FIRST[5])], mean.at[pl.ds(0, FIRST[5])]),
            ]
        )
    ]
    for copy in loads[:3]:
        copy.start()

    for m in range(1, 8):
        got8[m * 8 : (m + 1) * 8, :] = jnp.zeros((8, PACK), jnp.float32)

    barrier = pltpu.get_barrier_semaphore()
    for m in range(1, 8):
        pl.semaphore_signal(barrier, inc=1, device_id=peer(m), device_id_type=MESH)
    for bit in range(3, -1, -1):

        @pl.when(jnp.logical_not(upper(bit)))
        def _(bit=bit):
            for j in range(1 << bit, 2 << bit):
                pl.semaphore_signal(barrier, inc=1, device_id=peer(8 * j), device_id_type=MESH)

    def column_copy(j):
        level = level_of(j)
        rows = TOKENS_HERE >> level
        at = (level - 5) * 16 + (j - (1 << (level - 5))) * rows
        return pltpu.make_async_remote_copy(
            kvc.at[pl.ds(FIRST[level], rows)], kvz.at[pl.ds(at, rows)],
            z_send.at[j], z_recv.at[j], device_id=peer(8 * j), device_id_type=MESH,
        )

    def near_copy(i, src, dst, mask):
        return pltpu.make_async_remote_copy(
            src, dst, n_send.at[i], n_recv.at[i], device_id=peer(mask), device_id_type=MESH
        )

    near_copies = [
        near_copy(0, kvc.at[pl.ds(FIRST[2], 128)], kv2, 1),
        near_copy(1, kvc.at[pl.ds(FIRST[3], 64)], kv3.at[pl.ds(0, 64)], 2),
        near_copy(2, kvc.at[pl.ds(FIRST[4], 32)], kv4.at[pl.ds(0, 32)], 4),
        near_copy(3, kvc.at[pl.ds(FIRST[4], 32)], kv4.at[pl.ds(32, 32)], 6),
        near_copy(4, kv3.at[pl.ds(0, 64)], kv3.at[pl.ds(64, 64)], 1),
        near_copy(5, kv4.at[pl.ds(0, 64)], kv4.at[pl.ds(64, 64)], 1),
        near_copy(6, kvz.at[pl.ds(0, 32)], kvo.at[pl.ds(0, 32)], 1),
        near_copy(7, kvz.at[pl.ds(32, 16)], kvo.at[pl.ds(32, 16)], 1),
    ]

    def query_copy(m):
        if m % 2 == 0:
            src, dst = qg.at[pl.ds(0, SLOT)], qg.at[pl.ds(m // 2 * SLOT, SLOT)]
        else:
            src, dst = qg.at[pl.ds(24, 8)], q8.at[pl.ds(m // 2 * 8, 8)]
        return pltpu.make_async_remote_copy(
            src, dst, q_send.at[m], q_recv.at[m], device_id=peer(m), device_id_type=MESH
        )

    def return_copy(m):
        rows = pl.ds(m // 2 * SLOT + 24 * (m % 2), 8 if m % 2 else 24)
        return pltpu.make_async_remote_copy(
            ret.at[rows], got.at[rows],
            r_send.at[m], r_recv.at[m], device_id=peer(m - m % 2), device_id_type=MESH,
        )

    def last_copy(m):
        return pltpu.make_async_remote_copy(
            ret8.at[pl.ds(m * 8 + 4, 2)], got8.at[pl.ds(m * 8 + 4, 2)],
            e_send.at[m], e_recv.at[m], device_id=peer(m), device_id_type=MESH,
        )

    for copy in loads[:3]:
        copy.wait()
    for copy in (loads[5], loads[3], loads[4]):
        copy.start()
    far, close = slice(FIRST[5], COARSE), slice(0, FIRST[5])
    kvc[far, :WIDE] = jnp.dot(mean[far, :], k[...], preferred_element_type=jnp.float32)
    kvc[far, WIDE:] = jnp.dot(mean[far, :], v[...], preferred_element_type=jnp.float32)

    pl.semaphore_wait(barrier, 7 + z)
    for bit in range(3, -1, -1):

        @pl.when(upper(bit))
        def _(bit=bit):
            for j in range(1 << bit, 2 << bit):
                column_copy(j).start()

    loads[5].wait()
    kvc[close, :WIDE] = jnp.dot(mean[close, :], k[...], preferred_element_type=jnp.float32)
    kvc[close, WIDE:] = jnp.dot(mean[close, :], v[...], preferred_element_type=jnp.float32)
    for copy in near_copies[:4]:
        copy.start()
    loads[3].wait()
    loads[4].wait()
    qc[...] = jnp.dot(mean[:COARSE, :], q[...], preferred_element_type=jnp.float32)
    qg[0:SLOT, :] = qc[FIRST[5] : COARSE, :]
    for m in range(1, 8):
        query_copy(m).start()

    ones = jnp.ones((GROUP, DH), jnp.bfloat16)
    q_near, k_near, v_near = [], [], []
    for g in range(2):
        rows = slice(g * GROUP, (g + 1) * GROUP)
        pair = mean[COARSE : COARSE + 128, GROUP:]
        q_near.append(jnp.dot(pair, q[rows, :], preferred_element_type=jnp.float32))
        k_near.append(jnp.dot(pair, k[rows, :], preferred_element_type=jnp.float32))
        v_near.append(jnp.dot(pair, v[rows, :], preferred_element_type=jnp.float32))
    level1 = {}
    for g in range(2):
        rows = slice(g * GROUP, (g + 1) * GROUP)
        ordered = jnp.dot(
            mean[COARSE:, :GROUP], q[rows, :], preferred_element_type=jnp.float32
        ).astype(jnp.bfloat16)
        for h in range(HEADS):
            cols = head_cols(h)
            scores = contract_last(ordered[:, cols], k[rows, cols]) * SCALE
            top = jnp.max(scores, axis=1, keepdims=True)
            probs = jnp.exp(scores - top)
            high = probs.astype(jnp.bfloat16)
            low = (probs - high.astype(jnp.float32)).astype(jnp.bfloat16)
            wide = jnp.concatenate([v[rows, cols], ones], axis=1)
            both = jnp.dot(high, wide, preferred_element_type=jnp.float32) + jnp.dot(
                low, wide, preferred_element_type=jnp.float32
            )
            state[g, h, 0] = jnp.broadcast_to(top, (GROUP, DH))
            state[g, h, 1] = both[:, DH:]
            state[g, h, 2] = both[:, :DH]
            level1[g, h] = terms(
                q_near[g][:, cols], k_near[1 - g][:, cols], v_near[1 - g][:, cols], 2.0
            )

    def answer(bit, here):
        @pl.when(jnp.logical_and(here, jnp.logical_not(upper(bit))))
        def _():
            for j in range((2 << bit) - 1, (1 << bit) - 1, -1):
                column_copy(j).wait_recv()
                column_copy(j).start()

    for bit in range(2):
        answer(bit, z >= 0)
    answer(2, z >= 3)
    near_copies[1].wait_recv()
    near_copies[4].start()
    near_copies[2].wait_recv()
    near_copies[3].wait_recv()
    near_copies[5].start()

    near_copies[0].wait_recv()
    level2 = [
        terms(qc[0:128, head_cols(h)], kv2[:, head_cols(h)], kv2[:, head_cols(h + 2)], 4.0)
        for h in range(HEADS)
    ]
    near_copies[4].wait_recv()
    level3 = [
        terms(qc[128:192, head_cols(h)], kv3[:, head_cols(h)], kv3[:, head_cols(h + 2)], 8.0)
        for h in range(HEADS)
    ]
    near_copies[5].wait_recv()
    level4 = [
        terms(qc[192:224, head_cols(h)], kv4[:, head_cols(h)], kv4[:, head_cols(h + 2)], 16.0)
        for h in range(HEADS)
    ]
    answer(2, z < 3)
    for g in range(2):
        for h in range(HEADS):
            joined = tuple(x[g * 16 : (g + 1) * 16] for x in level4[h])
            joined = merge(tuple(x[g * 32 : (g + 1) * 32] for x in level3[h]), double(joined))
            joined = merge(tuple(x[g * 64 : (g + 1) * 64] for x in level2[h]), double(joined))
            joined = double(merge(level1[g, h], double(joined)))
            top, den, num = merge((state[g, h, 0], state[g, h, 1], state[g, h, 2]), joined)
            state[g, h, 0] = top
            state[g, h, 1] = den
            state[g, h, 2] = num

    def collect(bit):
        @pl.when(upper(bit))
        def _():
            for j in range((2 << bit) - 1, (1 << bit) - 1, -1):
                column_copy(j).wait_recv()

    def partial(level, queries, fields):
        return pack(
            [
                terms(
                    queries[:, head_cols(h)],
                    fields[:, head_cols(h)],
                    fields[:, head_cols(h + 2)],
                    float(2**level),
                )
                for h in range(HEADS)
            ]
        )

    answer(3, z >= 4)
    collect(0)
    collect(1)
    near_copies[6].start()
    for m in range(1, 8):
        query_copy(m).wait_recv()

    def return_level(bit):
        first, rows = ((0, 16), (16, 8), (24, 8))[bit]
        queries = jnp.concatenate(
            [qg[i * SLOT + first : i * SLOT + first + rows, :] for i in range(4)], axis=0
        )
        fields = jnp.concatenate(
            [kvz[16 * bit : 16 * bit + 16, :], kvo[16 * bit : 16 * bit + 16, :]], axis=0
        )
        result = partial(5 + bit, queries, fields)
        for i in range(4):
            ret[i * SLOT + first : i * SLOT + first + rows, :] = result[i * rows : (i + 1) * rows]

    near_copies[6].wait_recv()
    return_level(0)
    return_level(1)
    for m in (4, 2, 6):
        return_copy(m).start()
    collect(2)
    near_copies[7].start()
    near_copies[7].wait_recv()
    return_level(2)
    for m in (5, 3, 7):
        return_copy(m).start()
    answer(3, z < 4)
    collect(3)
    queries = []
    for m in range(8):
        queries.append(
            q8[m // 2 * 8 : m // 2 * 8 + 8, :]
            if m % 2
            else qg[m // 2 * SLOT + 24 : (m // 2 + 1) * SLOT, :]
        )
    ret8[...] = partial(8, jnp.concatenate(queries, axis=0), kvz[48:64, :])
    for m in (4, 5, 2, 3, 6, 7, 1):
        last_copy(m).start()
    for m in range(2, 8):
        return_copy(m).wait_recv()
    parts = combine([ret[0:SLOT, :]] + [got[i * SLOT : (i + 1) * SLOT, :] for i in range(1, 4)])
    spread = jnp.dot(spread_rows(), pack(parts), precision=HIGHEST, preferred_element_type=jnp.float32)
    for g in range(2):
        for h in range(HEADS):
            five, six, seven = (
                unpack(spread[16 * i + 8 * g : 16 * i + 8 * g + 8, :], h) for i in range(3)
            )
            joined = merge(five, merge(six, seven))
            for _ in range(5):
                joined = double(joined)
            top, den, num = merge((state[g, h, 0], state[g, h, 1], state[g, h, 2]), joined)
            state[g, h, 0] = top
            state[g, h, 1] = den
            state[g, h, 2] = num
    for j in range(1, 16):
        column_copy(j).wait_send()
    for copy in near_copies:
        copy.wait_send()
    for m in range(1, 8):
        query_copy(m).wait_send()
    for m in range(2, 8):
        return_copy(m).wait_send()
    for m in range(1, 8):
        last_copy(m).wait()
    parts = combine([ret8[0:8, :]] + [got8[m * 8 : (m + 1) * 8, :] for m in range(1, 8)])
    for g in range(2):
        attended = []
        for h in range(HEADS):
            row = tuple(x[4 + g : 5 + g, :] for x in parts[h])
            gap = row[0] - state[g, h, 0]
            small = jnp.exp(-jnp.abs(gap))
            wa = jnp.where(gap > 0.0, small, 1.0)
            wb = jnp.where(gap > 0.0, 1.0, small)
            inverse = 1.0 / (wa * state[g, h, 1] + wb * row[1])
            joined = (wa * inverse) * state[g, h, 2] + (wb * inverse) * row[2]
            attended.append(joined.astype(jnp.bfloat16))
        out_ref[g * GROUP : (g + 1) * GROUP, :] = jnp.dot(
            mean[COARSE:, :GROUP], jnp.concatenate(attended, axis=1), preferred_element_type=jnp.float32
        ).astype(jnp.bfloat16)


def on_device(queries, keys, values):
    mean = jnp.asarray(averaging(), jnp.bfloat16)
    f32, bf16 = jnp.float32, jnp.bfloat16
    whole = (TOKENS_HERE, WIDE)
    dma = pltpu.SemaphoreType.DMA
    return pl.pallas_call(
        kernel,
        out_shape=jax.ShapeDtypeStruct(whole, bf16),
        in_specs=[pl.BlockSpec(memory_space=pl.ANY)] * 4,
        out_specs=pl.BlockSpec(memory_space=pltpu.VMEM),
        scratch_shapes=[
            pltpu.VMEM(whole, bf16),
            pltpu.VMEM(whole, bf16),
            pltpu.VMEM(whole, bf16),
            pltpu.VMEM(mean.shape, bf16),
            pltpu.VMEM((COARSE, 2 * WIDE), f32),
            pltpu.VMEM((COARSE, WIDE), f32),
            pltpu.VMEM((128, 2 * WIDE), f32),
            pltpu.VMEM((128, 2 * WIDE), f32),
            pltpu.VMEM((128, 2 * WIDE), f32),
            pltpu.VMEM((64, 2 * WIDE), f32),
            pltpu.VMEM((48, 2 * WIDE), f32),
            pltpu.VMEM((4 * SLOT, WIDE), f32),
            pltpu.VMEM((32, WIDE), f32),
            pltpu.VMEM((4 * SLOT, PACK), f32),
            pltpu.VMEM((4 * SLOT, PACK), f32),
            pltpu.VMEM((64, PACK), f32),
            pltpu.VMEM((64, PACK), f32),
            pltpu.VMEM((2, HEADS, 3, GROUP, DH), f32),
            dma((6,)),
            dma((16,)),
            dma((16,)),
            dma((8,)),
            dma((8,)),
            dma((8,)),
            dma((8,)),
            dma((8,)),
            dma((8,)),
            dma((8,)),
            dma((8,)),
        ],
        compiler_params=pltpu.CompilerParams(
            collective_id=0, has_side_effects=True, vmem_limit_bytes=54900 * 1024
        ),
    )(queries, keys, values, mean)


def solution(mesh):
    in_specs = (P("ctx", "head"), P("ctx", "head"), P("ctx", "head"))
    return jax.shard_map(
        on_device, mesh=mesh, in_specs=in_specs, out_specs=P("ctx", "head"), check_vma=False
    )
```

```python
import jax
import jax.numpy as jnp
import numpy as np
from jax import lax
from jax.experimental import pallas as pl
from jax.experimental.pallas import tpu as pltpu
from jax.sharding import PartitionSpec as P

HEADS = 2
DH = 128
GROUP = 256
TOKENS_HERE = 512
WIDE = HEADS * DH
SCALE = DH ** (-0.5)
MESH = pl.DeviceIdType.MESH
HIGHEST = lax.Precision.HIGHEST

FIRST = {2: 0, 3: 128, 4: 192, 5: 224, 6: 240, 7: 248, 8: 252}
COARSE = 256
SLOT = 32
PACK = 3 * DH


def reverse(value, bits):
    out = 0
    for _ in range(bits):
        out = out * 2 + value % 2
        value //= 2
    return out


def averaging():
    order = np.zeros((GROUP, GROUP), np.float32)
    for row in range(GROUP):
        order[row, reverse(row, 8)] = 1.0
    near = np.zeros((GROUP // 2, GROUP), np.float32)
    for row in range(GROUP // 2):
        first = reverse(row, 7) * 2
        near[row, first : first + 2] = 0.5
    far = np.zeros((COARSE, TOKENS_HERE), np.float32)
    for level in range(2, 9):
        rows = GROUP >> level
        for group in range(2):
            for row in range(rows):
                first = group * GROUP + (reverse(row, 8 - level) << level)
                far[FIRST[level] + group * rows + row, first : first + (1 << level)] = 0.5**level
    return np.concatenate([far, np.concatenate([order, np.pad(near, ((0, 128), (0, 0)))], axis=1)])


def spread_rows():
    row = lax.broadcasted_iota(jnp.int32, (48, SLOT), 0)
    col = lax.broadcasted_iota(jnp.int32, (48, SLOT), 1)
    group = row % 16 // 8
    six = 16 + group * 4 + row % 4
    seven = 24 + group * 2 + row % 2
    source = jnp.where(row < 16, row, jnp.where(row < 32, six, seven))
    return jnp.where(source == col, 1.0, 0.0)


def contract_last(a, b, precision=None):
    return lax.dot_general(
        a, b, (((1,), (1,)), ((), ())), precision=precision, preferred_element_type=jnp.float32
    )


def halves(x):
    high = x.astype(jnp.bfloat16)
    return high, (x - high.astype(jnp.float32)).astype(jnp.bfloat16)


def scaled_halves(q):
    return jnp.concatenate(halves(q * SCALE), axis=1)


def terms(q, k, v, weight):
    keys = k.shape[0]
    q_both = q if q.dtype == jnp.bfloat16 else scaled_halves(q)
    k_high, k_low = halves(k)
    k_high = jnp.concatenate([k_high, k_high], axis=1)
    k_low = jnp.concatenate([k_low, k_low], axis=1)
    v_both = jnp.concatenate(halves(v), axis=1)
    if keys == DH:
        scores = contract_last(q_both, jnp.concatenate([k_high, k_low], axis=0))
        scores = scores[:, :DH] + scores[:, DH:]
    else:
        scores = contract_last(q_both, k_high) + contract_last(q_both, k_low)
    top = jnp.max(scores, axis=1, keepdims=True)
    probs = jnp.exp(scores - top)
    den = weight * jnp.sum(probs, axis=1, keepdims=True)
    p_high, p_low = halves(probs * weight)
    if keys == DH:
        p_both = jnp.concatenate([p_high, p_low], axis=1)
        num = jnp.dot(
            p_both,
            jnp.concatenate([v_both, v_both], axis=0),
            preferred_element_type=jnp.float32,
        )
    else:
        num = jnp.dot(p_high, v_both, preferred_element_type=jnp.float32) + jnp.dot(
            p_low, v_both, preferred_element_type=jnp.float32
        )
    return top, den, num[:, :DH] + num[:, DH:]


def merge(a, b):
    top = jnp.maximum(a[0], b[0])
    wa = jnp.exp(a[0] - top)
    wb = jnp.exp(b[0] - top)
    return top, wa * a[1] + wb * b[1], wa * a[2] + wb * b[2]


def double(a):
    return tuple(jnp.concatenate([x, x], axis=0) for x in a)


def head_cols(h):
    return slice(h * DH, (h + 1) * DH)


def pack(parts):
    (top0, den0, num0), (top1, den1, num1) = parts
    rows = num0.shape[0]
    lane = lax.broadcasted_iota(jnp.int32, (rows, DH), 1)
    stats = jnp.where(
        lane < 64, jnp.where(lane < 32, top0, den0), jnp.where(lane < 96, top1, den1)
    )
    return jnp.concatenate([num0, num1, stats], axis=1)


def unpack(x, h):
    at = WIDE + 64 * h
    return x[:, at : at + 1], x[:, at + 32 : at + 33], x[:, head_cols(h)]


def total(items):
    while len(items) > 1:
        items = [items[i] + items[i + 1] for i in range(0, len(items), 2)]
    return items[0]


def combine(slots):
    out = []
    for h in range(HEADS):
        parts = [unpack(x, h) for x in slots]
        tops = [p[0] for p in parts]
        while len(tops) > 1:
            tops = [jnp.maximum(tops[i], tops[i + 1]) for i in range(0, len(tops), 2)]
        scaled = [jnp.exp(p[0] - tops[0]) for p in parts]
        out.append(
            (
                tops[0],
                total([w * p[1] for w, p in zip(scaled, parts)]),
                total([w * p[2] for w, p in zip(scaled, parts)]),
            )
        )
    return out


def level_of(k):
    return 5 + (k.bit_length() - 1)


def kernel(
    q_hbm, k_hbm, v_hbm, mean_hbm, out_ref,
    q, k, v, mean,
    kvc, qc, kv2, kv3, kv4, kvz, kvo, qg, q8, ret, got, ret8, got8, state,
    load, z_send, z_recv, n_send, n_recv, q_send, q_recv, r_send, r_recv, e_send, e_recv,
):
    me = lax.axis_index("ctx")
    head = lax.axis_index("head")
    z = me // 8

    def peer(mask):
        return (jnp.bitwise_xor(me, mask), head)

    def upper(bit):
        return z // (1 << bit) % 2 == 1

    loads = [
        pltpu.make_async_copy(a, b, load.at[i])
        for i, (a, b) in enumerate(
            [
                (mean_hbm.at[pl.ds(FIRST[5], SLOT)], mean.at[pl.ds(FIRST[5], SLOT)]),
                (k_hbm, k),
                (v_hbm, v),
                (q_hbm, q),
                (mean_hbm.at[pl.ds(COARSE, COARSE)], mean.at[pl.ds(COARSE, COARSE)]),
                (mean_hbm.at[pl.ds(0, FIRST[5])], mean.at[pl.ds(0, FIRST[5])]),
            ]
        )
    ]
    for copy in loads[:3]:
        copy.start()

    for m in range(1, 8):
        got8[m * 8 : (m + 1) * 8, :] = jnp.zeros((8, PACK), jnp.float32)

    barrier = pltpu.get_barrier_semaphore()
    for m in range(1, 8):
        pl.semaphore_signal(barrier, inc=1, device_id=peer(m), device_id_type=MESH)
    for bit in range(3, -1, -1):

        @pl.when(jnp.logical_not(upper(bit)))
        def _(bit=bit):
            for j in range(1 << bit, 2 << bit):
                pl.semaphore_signal(barrier, inc=1, device_id=peer(8 * j), device_id_type=MESH)

    def column_copy(j):
        level = level_of(j)
        rows = TOKENS_HERE >> level
        at = (level - 5) * 16 + (j - (1 << (level - 5))) * rows
        return pltpu.make_async_remote_copy(
            kvc.at[pl.ds(FIRST[level], rows)], kvz.at[pl.ds(at, rows)],
            z_send.at[j], z_recv.at[j], device_id=peer(8 * j), device_id_type=MESH,
        )

    def near_copy(i, src, dst, mask):
        return pltpu.make_async_remote_copy(
            src, dst, n_send.at[i], n_recv.at[i], device_id=peer(mask), device_id_type=MESH
        )

    near_copies = [
        near_copy(0, kvc.at[pl.ds(FIRST[2], 128)], kv2, 1),
        near_copy(1, kvc.at[pl.ds(FIRST[3], 64)], kv3.at[pl.ds(0, 64)], 2),
        near_copy(2, kvc.at[pl.ds(FIRST[4], 32)], kv4.at[pl.ds(0, 32)], 4),
        near_copy(3, kvc.at[pl.ds(FIRST[4], 32)], kv4.at[pl.ds(32, 32)], 6),
        near_copy(4, kv3.at[pl.ds(0, 64)], kv3.at[pl.ds(64, 64)], 1),
        near_copy(5, kv4.at[pl.ds(0, 64)], kv4.at[pl.ds(64, 64)], 1),
        near_copy(6, kvz.at[pl.ds(0, 32)], kvo.at[pl.ds(0, 32)], 1),
        near_copy(7, kvz.at[pl.ds(32, 16)], kvo.at[pl.ds(32, 16)], 1),
    ]

    def query_copy(m):
        if m % 2 == 0:
            src, dst = qg.at[pl.ds(0, SLOT)], qg.at[pl.ds(m // 2 * SLOT, SLOT)]
        else:
            src, dst = qg.at[pl.ds(24, 8)], q8.at[pl.ds(m // 2 * 8, 8)]
        return pltpu.make_async_remote_copy(
            src, dst, q_send.at[m], q_recv.at[m], device_id=peer(m), device_id_type=MESH
        )

    def return_copy(m):
        rows = pl.ds(m // 2 * SLOT + 24 * (m % 2), 8 if m % 2 else 24)
        return pltpu.make_async_remote_copy(
            ret.at[rows], got.at[rows],
            r_send.at[m], r_recv.at[m], device_id=peer(m - m % 2), device_id_type=MESH,
        )

    def last_copy(m):
        return pltpu.make_async_remote_copy(
            ret8.at[pl.ds(m * 8 + 4, 2)], got8.at[pl.ds(m * 8 + 4, 2)],
            e_send.at[m], e_recv.at[m], device_id=peer(m), device_id_type=MESH,
        )

    for copy in loads[:3]:
        copy.wait()
    for copy in (loads[5], loads[3], loads[4]):
        copy.start()
    far, close = slice(FIRST[5], COARSE), slice(0, FIRST[5])
    kvc[far, :WIDE] = jnp.dot(mean[far, :], k[...], preferred_element_type=jnp.float32)
    kvc[far, WIDE:] = jnp.dot(mean[far, :], v[...], preferred_element_type=jnp.float32)

    pl.semaphore_wait(barrier, 7 + z)
    for bit in range(3, -1, -1):

        @pl.when(upper(bit))
        def _(bit=bit):
            for j in range(1 << bit, 2 << bit):
                column_copy(j).start()

    loads[5].wait()
    kvc[close, :WIDE] = jnp.dot(mean[close, :], k[...], preferred_element_type=jnp.float32)
    kvc[close, WIDE:] = jnp.dot(mean[close, :], v[...], preferred_element_type=jnp.float32)
    for copy in near_copies[:4]:
        copy.start()
    loads[3].wait()
    loads[4].wait()
    qc[...] = jnp.dot(mean[:COARSE, :], q[...], preferred_element_type=jnp.float32)
    qg[0:SLOT, :] = qc[FIRST[5] : COARSE, :]
    for m in range(1, 8):
        query_copy(m).start()

    ones = jnp.ones((GROUP, DH), jnp.bfloat16)
    q_near, k_near, v_near = [], [], []
    for g in range(2):
        rows = slice(g * GROUP, (g + 1) * GROUP)
        pair = mean[COARSE : COARSE + 128, GROUP:]
        q_near.append(jnp.dot(pair, q[rows, :], preferred_element_type=jnp.float32))
        k_near.append(jnp.dot(pair, k[rows, :], preferred_element_type=jnp.float32))
        v_near.append(jnp.dot(pair, v[rows, :], preferred_element_type=jnp.float32))
    level1 = {}
    for g in range(2):
        rows = slice(g * GROUP, (g + 1) * GROUP)
        ordered = jnp.dot(
            mean[COARSE:, :GROUP], q[rows, :], preferred_element_type=jnp.float32
        ).astype(jnp.bfloat16)
        for h in range(HEADS):
            cols = head_cols(h)
            scores = contract_last(ordered[:, cols], k[rows, cols]) * SCALE
            top = jnp.max(scores, axis=1, keepdims=True)
            probs = jnp.exp(scores - top)
            high = probs.astype(jnp.bfloat16)
            low = (probs - high.astype(jnp.float32)).astype(jnp.bfloat16)
            wide = jnp.concatenate([v[rows, cols], ones], axis=1)
            both = jnp.dot(high, wide, preferred_element_type=jnp.float32) + jnp.dot(
                low, wide, preferred_element_type=jnp.float32
            )
            state[g, h, 0] = jnp.broadcast_to(top, (GROUP, DH))
            state[g, h, 1] = both[:, DH:]
            state[g, h, 2] = both[:, :DH]
            level1[g, h] = terms(
                q_near[g][:, cols], k_near[1 - g][:, cols], v_near[1 - g][:, cols], 2.0
            )

    def answer(bit, here):
        @pl.when(jnp.logical_and(here, jnp.logical_not(upper(bit))))
        def _():
            for j in range((2 << bit) - 1, (1 << bit) - 1, -1):
                column_copy(j).wait_recv()
                column_copy(j).start()

    for bit in range(2):
        answer(bit, z >= 0)
    answer(2, z >= 3)
    near_copies[1].wait_recv()
    near_copies[4].start()
    near_copies[2].wait_recv()
    near_copies[3].wait_recv()
    near_copies[5].start()

    near_copies[0].wait_recv()
    level2 = [
        terms(qc[0:128, head_cols(h)], kv2[:, head_cols(h)], kv2[:, head_cols(h + 2)], 4.0)
        for h in range(HEADS)
    ]
    near_copies[4].wait_recv()
    level3 = [
        terms(qc[128:192, head_cols(h)], kv3[:, head_cols(h)], kv3[:, head_cols(h + 2)], 8.0)
        for h in range(HEADS)
    ]
    near_copies[5].wait_recv()
    level4 = [
        terms(qc[192:224, head_cols(h)], kv4[:, head_cols(h)], kv4[:, head_cols(h + 2)], 16.0)
        for h in range(HEADS)
    ]
    answer(2, z < 3)
    for g in range(2):
        for h in range(HEADS):
            joined = tuple(x[g * 16 : (g + 1) * 16] for x in level4[h])
            joined = merge(tuple(x[g * 32 : (g + 1) * 32] for x in level3[h]), double(joined))
            joined = merge(tuple(x[g * 64 : (g + 1) * 64] for x in level2[h]), double(joined))
            joined = double(merge(level1[g, h], double(joined)))
            top, den, num = merge((state[g, h, 0], state[g, h, 1], state[g, h, 2]), joined)
            state[g, h, 0] = top
            state[g, h, 1] = den
            state[g, h, 2] = num

    def collect(bit):
        @pl.when(upper(bit))
        def _():
            for j in range((2 << bit) - 1, (1 << bit) - 1, -1):
                column_copy(j).wait_recv()

    def partial(level, queries, fields):
        return pack(
            [
                terms(
                    queries[:, head_cols(h)],
                    fields[:, head_cols(h)],
                    fields[:, head_cols(h + 2)],
                    float(2**level),
                )
                for h in range(HEADS)
            ]
        )

    answer(3, z >= 4)
    collect(0)
    collect(1)
    near_copies[6].start()
    for m in range(1, 8):
        query_copy(m).wait_recv()

    def return_level(bit):
        first, rows = ((0, 16), (16, 8), (24, 8))[bit]
        queries = jnp.concatenate(
            [qg[i * SLOT + first : i * SLOT + first + rows, :] for i in range(4)], axis=0
        )
        fields = jnp.concatenate(
            [kvz[16 * bit : 16 * bit + 16, :], kvo[16 * bit : 16 * bit + 16, :]], axis=0
        )
        result = partial(5 + bit, queries, fields)
        for i in range(4):
            ret[i * SLOT + first : i * SLOT + first + rows, :] = result[i * rows : (i + 1) * rows]

    near_copies[6].wait_recv()
    return_level(0)
    return_level(1)
    for m in (4, 2, 6):
        return_copy(m).start()
    collect(2)
    near_copies[7].start()
    near_copies[7].wait_recv()
    return_level(2)
    for m in (5, 3, 7):
        return_copy(m).start()
    queries = []
    for m in range(8):
        queries.append(
            q8[m // 2 * 8 : m // 2 * 8 + 8, :]
            if m % 2
            else qg[m // 2 * SLOT + 24 : (m // 2 + 1) * SLOT, :]
        )
    queries = jnp.concatenate(queries, axis=0)
    last_q = [scaled_halves(queries[:, head_cols(h)]) for h in range(HEADS)]
    answer(3, z < 4)
    collect(3)
    ret8[...] = pack(
        [
            terms(last_q[h], kvz[48:64, head_cols(h)], kvz[48:64, head_cols(h + 2)], 256.0)
            for h in range(HEADS)
        ]
    )
    for m in (4, 5, 2, 3, 6, 7, 1):
        last_copy(m).start()
    for m in range(2, 8):
        return_copy(m).wait_recv()
    parts = combine([ret[0:SLOT, :]] + [got[i * SLOT : (i + 1) * SLOT, :] for i in range(1, 4)])
    spread = jnp.dot(spread_rows(), pack(parts), precision=HIGHEST, preferred_element_type=jnp.float32)
    for g in range(2):
        for h in range(HEADS):
            five, six, seven = (
                unpack(spread[16 * i + 8 * g : 16 * i + 8 * g + 8, :], h) for i in range(3)
            )
            joined = merge(five, merge(six, seven))
            for _ in range(5):
                joined = double(joined)
            top, den, num = merge((state[g, h, 0], state[g, h, 1], state[g, h, 2]), joined)
            state[g, h, 0] = top
            state[g, h, 1] = den
            state[g, h, 2] = num
    for j in range(1, 16):
        column_copy(j).wait_send()
    for copy in near_copies:
        copy.wait_send()
    for m in range(1, 8):
        query_copy(m).wait_send()
    for m in range(2, 8):
        return_copy(m).wait_send()
    for m in range(1, 8):
        last_copy(m).wait()
    parts = combine([ret8[0:8, :]] + [got8[m * 8 : (m + 1) * 8, :] for m in range(1, 8)])
    for g in range(2):
        attended = []
        for h in range(HEADS):
            row = tuple(x[4 + g : 5 + g, :] for x in parts[h])
            gap = row[0] - state[g, h, 0]
            small = jnp.exp(-jnp.abs(gap))
            wa = jnp.where(gap > 0.0, small, 1.0)
            wb = jnp.where(gap > 0.0, 1.0, small)
            inverse = 1.0 / (wa * state[g, h, 1] + wb * row[1])
            joined = (wa * inverse) * state[g, h, 2] + (wb * inverse) * row[2]
            attended.append(joined.astype(jnp.bfloat16))
        out_ref[g * GROUP : (g + 1) * GROUP, :] = jnp.dot(
            mean[COARSE:, :GROUP], jnp.concatenate(attended, axis=1), preferred_element_type=jnp.float32
        ).astype(jnp.bfloat16)


def on_device(queries, keys, values):
    mean = jnp.asarray(averaging(), jnp.bfloat16)
    f32, bf16 = jnp.float32, jnp.bfloat16
    whole = (TOKENS_HERE, WIDE)
    dma = pltpu.SemaphoreType.DMA
    return pl.pallas_call(
        kernel,
        out_shape=jax.ShapeDtypeStruct(whole, bf16),
        in_specs=[pl.BlockSpec(memory_space=pl.ANY)] * 4,
        out_specs=pl.BlockSpec(memory_space=pltpu.VMEM),
        scratch_shapes=[
            pltpu.VMEM(whole, bf16),
            pltpu.VMEM(whole, bf16),
            pltpu.VMEM(whole, bf16),
            pltpu.VMEM(mean.shape, bf16),
            pltpu.VMEM((COARSE, 2 * WIDE), f32),
            pltpu.VMEM((COARSE, WIDE), f32),
            pltpu.VMEM((128, 2 * WIDE), f32),
            pltpu.VMEM((128, 2 * WIDE), f32),
            pltpu.VMEM((128, 2 * WIDE), f32),
            pltpu.VMEM((64, 2 * WIDE), f32),
            pltpu.VMEM((48, 2 * WIDE), f32),
            pltpu.VMEM((4 * SLOT, WIDE), f32),
            pltpu.VMEM((32, WIDE), f32),
            pltpu.VMEM((4 * SLOT, PACK), f32),
            pltpu.VMEM((4 * SLOT, PACK), f32),
            pltpu.VMEM((64, PACK), f32),
            pltpu.VMEM((64, PACK), f32),
            pltpu.VMEM((2, HEADS, 3, GROUP, DH), f32),
            dma((6,)),
            dma((16,)),
            dma((16,)),
            dma((8,)),
            dma((8,)),
            dma((8,)),
            dma((8,)),
            dma((8,)),
            dma((8,)),
            dma((8,)),
            dma((8,)),
        ],
        compiler_params=pltpu.CompilerParams(
            collective_id=0, has_side_effects=True, vmem_limit_bytes=54900 * 1024
        ),
    )(queries, keys, values, mean)


def solution(mesh):
    in_specs = (P("ctx", "head"), P("ctx", "head"), P("ctx", "head"))
    return jax.shard_map(
        on_device, mesh=mesh, in_specs=in_specs, out_specs=P("ctx", "head"), check_vma=False
    )
```
